128 devices in a mesh: row: 4 (over z), col: 32 (over x, y, core).
Axes of the slice: x: 4, y: 4, z: 4, core: 2. Of those that a mesh axis runs over, the one named last changes fastest.
Arguments:
- tokens: bfloat16 [32768, 1024], P(('row', 'col')), may hold values from -6 to 6
- out_grad: bfloat16 [32768, 1024], P(('row', 'col')), may hold values from -6 to 6
- expert_ids: int32 [32768], P(('row', 'col')), may hold values from 0 to 127, as said below
- router_logits: float32 [32768, 128], P(('row', 'col')), may hold values from -6 to 273
- router_weight: bfloat16 [128, 1024], P(('row', 'col')), may hold values from -0.1875 to 0.1875
- w_in: bfloat16 [128, 1024, 2048], P(('row', 'col')), may hold values from -0.1875 to 0.1875
- w_out: bfloat16 [128, 2048, 1024], P(('row', 'col')), may hold values from -0.125 to 0.125
Outputs:
- d_tokens: bfloat16 [32768, 1024], P(('row', 'col'))
- d_w_in: bfloat16 [128, 1024, 2048], P(('row', 'col'))
- d_w_out: bfloat16 [128, 2048, 1024], P(('row', 'col'))
- d_router: float32 [128, 1024], P(('row', 'col'))
The draws below stay inside these ranges and needn't reach their ends.
Inputs may be any that keep to these rules, and one draw needn't show every extreme that they name: `expert_ids`: among the 256 tokens of one device no expert is chosen more than 4 times, and one expert is chosen exactly 4 times by the tokens of every device.
All inputs are finite; a program needn't handle non-finite values.
Results may differ from the reference program's by a relative error of at most 0.017.
Values may be sent and summed in bfloat16 or wider, within the bound.
No kernel may reach another device: no remote copies, remote signals or barrier semaphores. Data moves between devices by JAX's collectives and lax.ppermute only.
A program may use at most 128 MiB of HBM per device.

```python
import jax
import jax.numpy as jnp
from jax import lax

D = 1024
F = 2048
TOK_DEV = 256
EXPERTS = 128
CAP = 4
TOKENS = 32768


def route_table(key):
    sources = TOKENS // TOK_DEV
    slots = EXPERTS * CAP
    popular = jax.random.permutation(jax.random.fold_in(key, 11), EXPERTS).astype(jnp.int32)
    slot_expert = jnp.arange(slots, dtype=jnp.int32) // CAP

    def one_source(index):
        source_key = jax.random.fold_in(jax.random.fold_in(key, 12), index)
        noise = jax.random.randint(source_key, (slots,), 0, 1024, dtype=jnp.int32)
        score = noise + popular[slot_expert] * 8
        score = jnp.where(popular[slot_expert] == 0, -1, score) + 1
        order = jnp.argsort(score * slots + jnp.arange(slots, dtype=jnp.int32), stable=True)
        picked = slot_expert[order[:TOK_DEV]]
        shuffle = jax.random.permutation(jax.random.fold_in(source_key, 1), TOK_DEV)
        return picked[shuffle]
    return jax.vmap(one_source)(jnp.arange(sources, dtype=jnp.int32)).reshape(TOKENS).astype(jnp.int32)


def draw_expert_ids(key, part):
    return route_table(key)


def draw_router_logits(key, part):
    chosen_ids = route_table(key)
    key = jax.random.fold_in(key, 5)
    keys = jax.random.split(key, 2)
    base = jnp.clip(1.5 * jax.random.normal(keys[0], (TOKENS, EXPERTS), jnp.float32), -6.0, 6.0)
    columns = jnp.arange(EXPERTS, dtype=jnp.int32)[None, :]
    chosen = (chosen_ids[:, None] == columns).astype(jnp.float32)
    boost = jax.random.uniform(keys[1], (TOKENS, 1), jnp.float32, 3.0, 7.0)
    logits = base + boost * chosen
    return logits.astype(jnp.float32)


def block_scale(own_key, dims, shards, least, top_value):
    level, own = 1.0, jax.random.fold_in(own_key, 6)
    for position, shards_of in shards:
        heights = jnp.exp(jax.random.uniform(jax.random.fold_in(own, position), (shards_of,), jnp.float32, least / len(shards), top_value / len(shards)))
        level = level * jnp.repeat(heights, dims[position] // shards_of).reshape([-1 if axis == position else 1 for axis in range(len(dims))])
    return level


def centred(own_key, extent, scale, bound, cuts=(), held_as=jnp.bfloat16):
    gain = block_scale(own_key, extent, cuts, -0.22, 0.18) if cuts else 1.0
    array = jax.random.normal(own_key, extent, jnp.float32) * scale * gain
    return jnp.minimum(jnp.maximum(array, -bound), bound).astype(held_as)


def setup_inputs(seed: int = 0) -> dict:
    seeds = jax.random.split(jax.random.key(seed), 8)
    return {
        "tokens": centred(seeds[0], (TOKENS, D), 1.0, 6.0, ((0, 128),)),
        "out_grad": centred(seeds[1], (TOKENS, D), 1.0, 6.0, ((0, 128),)),
        "expert_ids": draw_expert_ids(jax.random.fold_in(seeds[7], 71), 0),
        "router_logits": draw_router_logits(jax.random.fold_in(seeds[7], 71), 0),
        "router_weight": centred(seeds[4], (EXPERTS, D), D ** -0.5, 0.1875, ((0, 128),)),
        "w_in": centred(seeds[5], (EXPERTS, D, F), D ** -0.5, 0.1875, ((0, 128),)),
        "w_out": centred(seeds[6], (EXPERTS, F, D), F ** -0.5, 0.125, ((0, 128),)),
    }


def reference(tokens, out_grad, expert_ids, router_logits, router_weight, w_in, w_out):
    sources = TOKENS // TOK_DEV
    slots = EXPERTS * CAP
    grouped = expert_ids.reshape(sources, TOK_DEV).astype(jnp.int32)
    onehot = (grouped[:, :, None] == jnp.arange(EXPERTS, dtype=jnp.int32)[None, None, :]).astype(jnp.int32)
    earlier = jnp.cumsum(onehot, axis=1) - onehot
    ranks = jnp.sum(earlier * onehot, axis=2)
    slot = grouped * CAP + ranks
    flat_slot = (jnp.arange(sources, dtype=jnp.int32)[:, None] * slots + slot).reshape(TOKENS).astype(jnp.int32)
    probs = jax.nn.softmax(router_logits.astype(jnp.float32), axis=-1)
    chosen = (expert_ids[:, None] == jnp.arange(EXPERTS, dtype=jnp.int32)[None, :]).astype(jnp.float32)
    gate = jnp.sum(probs * chosen, axis=1)
    scaled = (gate[:, None] * out_grad.astype(jnp.float32)).astype(jnp.bfloat16)
    routed_all = jnp.zeros((sources * slots, D), jnp.bfloat16).at[flat_slot].set(tokens)
    scaled_all = jnp.zeros((sources * slots, D), jnp.bfloat16).at[flat_slot].set(scaled)
    routed_all = routed_all.reshape(sources, EXPERTS, CAP, D).transpose(1, 0, 2, 3).reshape(EXPERTS, sources * CAP, D)
    scaled_all = scaled_all.reshape(sources, EXPERTS, CAP, D).transpose(1, 0, 2, 3).reshape(EXPERTS, sources * CAP, D)

    def expert(operands):
        routed, scaled_rows, inner_weight, outer_weight = operands
        pre_act = jnp.dot(routed, inner_weight, preferred_element_type=jnp.float32)
        hidden = jnp.maximum(pre_act, 0.0).astype(jnp.bfloat16)
        expert_out = jnp.dot(hidden, outer_weight, preferred_element_type=jnp.float32).astype(jnp.bfloat16)
        back = jnp.dot(scaled_rows, outer_weight.T, preferred_element_type=jnp.float32)
        hidden_grad = jnp.where(pre_act > 0.0, back, 0.0).astype(jnp.bfloat16)
        grad_in = jnp.dot(hidden_grad, inner_weight.T, preferred_element_type=jnp.float32).astype(jnp.bfloat16)
        grad_inner = jnp.dot(routed.T, hidden_grad, preferred_element_type=jnp.float32).astype(jnp.bfloat16)
        grad_outer = jnp.dot(hidden.T, scaled_rows, preferred_element_type=jnp.float32).astype(jnp.bfloat16)
        return grad_in, expert_out, grad_inner, grad_outer

    grad_in, expert_out, d_w_in, d_w_out = lax.map(expert, (routed_all, scaled_all, w_in, w_out))
    grad_in = grad_in.reshape(EXPERTS, sources, CAP, D).transpose(1, 0, 2, 3).reshape(sources * slots, D)
    expert_out = expert_out.reshape(EXPERTS, sources, CAP, D).transpose(1, 0, 2, 3).reshape(sources * slots, D)
    back_in = grad_in[flat_slot]
    back_out = expert_out[flat_slot]
    gate_grad = jnp.sum(out_grad.astype(jnp.float32) * back_out.astype(jnp.float32), axis=1)
    logit_grad = ((gate_grad * gate)[:, None] * (chosen - probs)).astype(jnp.bfloat16)
    d_router = jnp.dot(logit_grad.T, tokens, preferred_element_type=jnp.float32)
    router_part = jnp.dot(logit_grad, router_weight, preferred_element_type=jnp.float32)
    d_tokens = (back_in.astype(jnp.float32) + router_part).astype(jnp.bfloat16)
    return d_tokens, d_w_in, d_w_out, d_router
```

```python
import jax
import jax.numpy as jnp
from jax import lax
from jax.experimental import pallas as pl
from jax.experimental.pallas import tpu as pltpu
from jax.sharding import PartitionSpec as P

BF16 = jnp.bfloat16
F32 = jnp.float32
AXES = ("row", "col")
CAP = 4
EXTRA = 256
VMEM_LIMIT = 48 * 1024 * 1024


def dot(a, b, ca=1, cb=0):
    return lax.dot_general(a, b, (((ca,), (cb,)), ((), ())), preferred_element_type=F32)


def iota(shape, axis):
    return lax.broadcasted_iota(jnp.int32, shape, axis)


def prep_kernel(ids_ref, logits_ref, tok_ref, og_ref, rw_ref, send_ref, slot_ref, rhs_ref, extra_ref):
    step = pl.program_id(0)
    n_tok, width = tok_ref.shape
    experts = logits_ref.shape[1]
    rows = send_ref.shape[0]

    @pl.when(step == 0)
    def _():
        ids = ids_ref[...]
        onehot_t = jnp.where(iota((experts, n_tok), 0) == ids, 1.0, 0.0).astype(F32)
        upper = jnp.where(iota((n_tok, n_tok), 0) < iota((n_tok, n_tok), 1), 1.0, 0.0)
        earlier = dot(onehot_t.astype(BF16), upper.astype(BF16))
        rank = jnp.sum(earlier * onehot_t, axis=0, keepdims=True)
        slot_ref[...] = ids * (2 * CAP) + rank.astype(jnp.int32)
        onehot = onehot_t.T
        logits = logits_ref[...]
        grown = jnp.exp(logits - jnp.max(logits, axis=1, keepdims=True))
        probs = grown / jnp.sum(grown, axis=1, keepdims=True)
        gate = jnp.sum(probs * onehot, axis=1, keepdims=True)
        rhs_ref[pl.ds(0, n_tok), :] = tok_ref[...]
        rhs_ref[pl.ds(n_tok, n_tok), :] = (gate * og_ref[...].astype(F32)).astype(BF16)
        extra_ref[:, 0:experts] = (onehot - probs).astype(BF16)
        extra_ref[:, experts:] = jnp.zeros((n_tok, EXTRA - experts), BF16)

    slot = slot_ref[...]
    row = iota((rows, n_tok), 0) + step * rows
    first = jnp.where(row == slot, 1.0, 0.0).astype(BF16)
    second = jnp.where(row == slot + CAP, 1.0, 0.0).astype(BF16)
    both = jnp.concatenate([first, second], axis=1)
    send_ref[:, 0:width] = dot(both, rhs_ref[...]).astype(BF16)
    router = rw_ref[...].astype(F32)
    place = iota((2 * CAP, EXTRA), 0)
    pieces = jnp.zeros((2 * CAP, EXTRA), F32)
    for k in range(width // EXTRA):
        piece = jnp.broadcast_to(router[:, k * EXTRA : (k + 1) * EXTRA], (2 * CAP, EXTRA))
        pieces = jnp.where(place == k, piece, pieces)
    side = dot(second, extra_ref[...]).reshape(rows // (2 * CAP), 2 * CAP, EXTRA)
    side = side + pieces[None]
    send_ref[:, width:] = side.reshape(rows, EXTRA).astype(BF16)


def prep(ids, logits, tokens, out_grad, router_weight):
    n_tok, width = tokens.shape
    experts = logits.shape[1]
    rows = experts * 2 * CAP
    steps = 4
    whole = lambda i: (0, 0)
    return pl.pallas_call(
        prep_kernel,
        grid=(steps,),
        out_shape=(
            jax.ShapeDtypeStruct((rows, width + EXTRA), BF16),
            jax.ShapeDtypeStruct((1, n_tok), jnp.int32),
        ),
        in_specs=[
            pl.BlockSpec((1, n_tok), whole),
            pl.BlockSpec((n_tok, experts), whole),
            pl.BlockSpec((n_tok, width), whole),
            pl.BlockSpec((n_tok, width), whole),
            pl.BlockSpec((1, width), whole),
        ],
        out_specs=(
            pl.BlockSpec((rows // steps, width + EXTRA), lambda i: (i, 0)),
            pl.BlockSpec((1, n_tok), whole),
        ),
        scratch_shapes=[
            pltpu.VMEM((2 * n_tok, width), BF16),
            pltpu.VMEM((n_tok, EXTRA), BF16),
        ],
        compiler_params=pltpu.CompilerParams(vmem_limit_bytes=VMEM_LIMIT),
    )(ids, logits, tokens, out_grad, router_weight)


def split_halves(block):
    rows, columns = block.shape
    tiles = block.astype(F32).reshape(rows // 16, 2, 8, columns)
    even, odd = tiles[:, 0], tiles[:, 1]
    low = iota(even.shape, 1) < 4
    first = jnp.where(low, even, pltpu.roll(odd, 4, axis=1))
    second = jnp.where(low, pltpu.roll(even, 4, axis=1), odd)
    return first.reshape(rows // 2, columns).astype(BF16), second.reshape(rows // 2, columns).astype(BF16)


def join_halves(first, second):
    rows, columns = first.shape
    a = first.reshape(rows // 8, 8, columns)
    b = second.reshape(rows // 8, 8, columns)
    low = iota(a.shape, 1) < 4
    even = jnp.where(low, a, pltpu.roll(b, 4, axis=1))
    odd = jnp.where(low, pltpu.roll(a, 4, axis=1), b)
    return jnp.stack([even, odd], axis=1).reshape(2 * rows, columns)


def expert_kernel(
    recv_ref, w_in_ref, w_out_ref, back_ref, routed_ref, scaled_ref, hidden_ref, hgrad_ref,
    gi_ref, c_ref, part_ref,
):
    step = pl.program_id(0)
    last = pl.num_programs(0) - 1
    rows = routed_ref.shape[0]
    width = w_in_ref.shape[0]
    experts = rows // CAP

    @pl.when(step == 0)
    def _():
        for k in range(0, width + EXTRA, 256):
            first, second = split_halves(recv_ref[:, k : k + 256])
            routed_ref[:, k : k + 256] = first
            scaled_ref[:, k : k + 256] = second

    routed = routed_ref[:, 0:width]
    pre = dot(routed, w_in_ref[...])
    back = dot(scaled_ref[:, 0:width], w_out_ref[...], 1, 1)
    active = pre > 0.0
    hidden = jnp.maximum(pre, 0.0)
    hgrad = jnp.where(active, back, 0.0)
    hidden_ref[...] = hidden.astype(BF16)
    hgrad = hgrad.astype(BF16)
    hgrad_ref[...] = hgrad
    c = jnp.sum(hidden * back, axis=1, keepdims=True)
    gi = dot(hgrad, w_in_ref[...], 1, 1)

    @pl.when(step == 0)
    def _():
        gi_ref[...] = gi
        c_ref[...] = c

    @pl.when(step > 0)
    def _():
        gi_ref[...] += gi
        c_ref[...] += c

    @pl.when(step == last)
    def _():
        q = scaled_ref[:, width : width + experts].astype(F32)
        logit_grad = (c_ref[...] * q).astype(BF16)
        pieces = routed_ref[:, width : width + EXTRA]
        for k in range(width // EXTRA):
            pick = jnp.where(iota((experts, rows), 1) == iota((experts, rows), 0) * CAP + k, 1.0, 0.0)
            router = dot(pick.astype(BF16), pieces).astype(BF16)
            gi_ref[:, k * EXTRA : (k + 1) * EXTRA] += dot(logit_grad, router)
        half = width // 2
        for k in range(0, half, 256):
            joined = join_halves(gi_ref[:, k : k + 256], gi_ref[:, half + k : half + k + 256])
            back_ref[:, k : k + 256] = joined.astype(BF16)
        part = dot(logit_grad, routed, 0, 0)
        for k in range(width // 128):
            part_ref[pl.ds(k, experts, stride=8), :] = part[:, k * 128 : (k + 1) * 128]
        back_ref[:, half:] = part_ref[...].astype(BF16)


def expert(recv, w_in, w_out):
    rows2, columns = recv.shape
    rows = rows2 // 2
    width, inner = w_in.shape
    experts = rows // CAP
    block = 512
    whole = lambda i: (0, 0)
    return pl.pallas_call(
        expert_kernel,
        grid=(inner // block,),
        out_shape=(
            jax.ShapeDtypeStruct((rows2, width // 2 + 128), BF16),
            jax.ShapeDtypeStruct((rows, columns), BF16),
            jax.ShapeDtypeStruct((rows, columns), BF16),
            jax.ShapeDtypeStruct((rows, inner), BF16),
            jax.ShapeDtypeStruct((rows, inner), BF16),
        ),
        in_specs=[
            pl.BlockSpec((rows2, columns), whole),
            pl.BlockSpec((width, block), lambda i: (0, i)),
            pl.BlockSpec((block, width), lambda i: (i, 0)),
        ],
        out_specs=(
            pl.BlockSpec((rows2, width // 2 + 128), whole),
            pl.BlockSpec((rows, columns), whole),
            pl.BlockSpec((rows, columns), whole),
            pl.BlockSpec((rows, block), lambda i: (0, i)),
            pl.BlockSpec((rows, block), lambda i: (0, i)),
        ),
        scratch_shapes=[
            pltpu.VMEM((rows, width), F32),
            pltpu.VMEM((rows, 1), F32),
            pltpu.VMEM((experts * 8, 128), F32),
        ],
        compiler_params=pltpu.CompilerParams(vmem_limit_bytes=VMEM_LIMIT),
    )(recv, w_in, w_out)


def weight_kernel(routed_ref, scaled_ref, hidden_ref, hgrad_ref, d_in_ref, d_out_ref):
    width = d_in_ref.shape[0]
    d_in_ref[...] = dot(routed_ref[:, 0:width], hgrad_ref[...], 0, 0).astype(BF16)
    d_out_ref[...] = dot(hidden_ref[...], scaled_ref[:, 0:width], 0, 0).astype(BF16)


def weight_grads(routed, scaled, hidden, hgrad, width):
    rows, inner = hidden.shape
    block = 512
    whole = lambda i: (0, 0)
    flops = 2 * 2 * rows * inner * width
    moved = 2 * (2 * rows * inner + 2 * rows * width + 2 * inner * width)
    return pl.pallas_call(
        weight_kernel,
        grid=(inner // block,),
        out_shape=(
            jax.ShapeDtypeStruct((width, inner), BF16),
            jax.ShapeDtypeStruct((inner, width), BF16),
        ),
        in_specs=[
            pl.BlockSpec(routed.shape, whole),
            pl.BlockSpec(scaled.shape, whole),
            pl.BlockSpec((rows, block), lambda i: (0, i)),
            pl.BlockSpec((rows, block), lambda i: (0, i)),
        ],
        out_specs=(
            pl.BlockSpec((width, block), lambda i: (0, i)),
            pl.BlockSpec((block, width), lambda i: (i, 0)),
        ),
        compiler_params=pltpu.CompilerParams(vmem_limit_bytes=VMEM_LIMIT),
        cost_estimate=pl.CostEstimate(flops=flops, bytes_accessed=moved, transcendentals=0),
    )(routed, scaled, hidden, hgrad)


def post_kernel(recv_ref, slot_ref, d_tok_ref, d_router_ref):
    rows = recv_ref.shape[0]
    n_tok, width = d_tok_ref.shape
    half = width // 2
    row = iota((rows, n_tok), 0)
    slot = slot_ref[...]
    first = jnp.where(row == slot, 1.0, 0.0).astype(BF16)
    second = jnp.where(row == slot + CAP, 1.0, 0.0).astype(BF16)
    d_tok_ref[:, 0:half] = dot(first, recv_ref[:, 0:half], 0, 0).astype(BF16)
    d_tok_ref[:, half:] = dot(second, recv_ref[:, 0:half], 0, 0).astype(BF16)
    parts = recv_ref[:, half:].astype(F32).reshape(rows // 8, 8, 128)
    total = jnp.sum(parts, axis=0)
    for k in range(width // 128):
        d_router_ref[:, k * 128 : (k + 1) * 128] = total[k : k + 1, :]


def post(recv, slot, n_tok, width):
    return pl.pallas_call(
        post_kernel,
        out_shape=(
            jax.ShapeDtypeStruct((n_tok, width), BF16),
            jax.ShapeDtypeStruct((1, width), F32),
        ),
        compiler_params=pltpu.CompilerParams(vmem_limit_bytes=VMEM_LIMIT),
    )(recv, slot)


def exchange(rows, experts):
    count, columns = rows.shape
    cut = rows.reshape(experts, count // experts, columns)
    return lax.all_to_all(cut, AXES, split_axis=0, concat_axis=0, tiled=True).reshape(count, columns)


def per_device(tokens, out_grad, expert_ids, router_logits, router_weight, w_in, w_out):
    experts = router_logits.shape[1]
    n_tok, width = tokens.shape
    send, slot = prep(expert_ids.reshape(1, n_tok), router_logits, tokens, out_grad, router_weight)
    recv = exchange(send, experts)
    ret, routed, scaled, hidden, hgrad = expert(recv, w_in[0], w_out[0])
    got = exchange(ret, experts)
    d_in, d_out = weight_grads(routed, scaled, hidden, hgrad, width)
    d_tokens, d_router = post(got, slot, n_tok, width)
    return (d_tokens, d_in[None], d_out[None], d_router)


def solution(mesh):
    rows = P(AXES, None)
    cube = P(AXES, None, None)
    return jax.shard_map(
        per_device,
        mesh=mesh,
        in_specs=(rows, rows, P(AXES), rows, rows, cube, cube),
        out_specs=(rows, cube, cube, rows),
        check_vma=False,
    )
```

```python
import jax
import jax.numpy as jnp
from jax import lax
from jax.experimental import pallas as pl
from jax.experimental.pallas import tpu as pltpu
from jax.sharding import PartitionSpec as P

BF16 = jnp.bfloat16
F32 = jnp.float32
AXES = ("row", "col")
CAP = 4
EXTRA = 256
MIB = 1024 * 1024
PREP_VMEM = 63 * MIB
EXPERT_VMEM = 56 * MIB
VMEM_LIMIT = 48 * MIB
BLOCKS = 4


def dot(a, b, ca=1, cb=0):
    return lax.dot_general(a, b, (((ca,), (cb,)), ((), ())), preferred_element_type=F32)


def iota(shape, axis):
    return lax.broadcasted_iota(jnp.int32, shape, axis)


def prep_kernel(
    ids_hbm, logits_hbm, tok_hbm, og_hbm, rw_hbm, send_hbm, slot_ref,
    ids_ref, logits_ref, rhs_ref, og_ref, rw_ref, extra_ref, send_ref, sems, out_sems,
):
    n_tok, width = og_ref.shape
    experts = logits_ref.shape[1]
    rows = send_ref.shape[0]
    copies = [
        pltpu.make_async_copy(src, dst, sems.at[i])
        for i, (src, dst) in enumerate(
            [
                (ids_hbm, ids_ref),
                (logits_hbm, logits_ref),
                (og_hbm, og_ref),
                (tok_hbm, rhs_ref.at[pl.ds(0, n_tok), :]),
                (rw_hbm, rw_ref),
            ]
        )
    ]
    for copy in copies:
        copy.start()
    upper = jnp.where(iota((n_tok, n_tok), 0) < iota((n_tok, n_tok), 1), 1.0, 0.0).astype(BF16)
    copies[0].wait()
    ids = ids_ref[...]
    onehot_t = jnp.where(iota((experts, n_tok), 0) == ids, 1.0, 0.0).astype(F32)
    earlier = dot(onehot_t.astype(BF16), upper)
    rank = jnp.sum(earlier * onehot_t, axis=0, keepdims=True)
    slot = ids * (2 * CAP) + rank.astype(jnp.int32)
    slot_ref[...] = slot
    onehot = onehot_t.T
    copies[1].wait()
    logits = logits_ref[...]
    grown = jnp.exp(logits - jnp.max(logits, axis=1, keepdims=True))
    probs = grown / jnp.sum(grown, axis=1, keepdims=True)
    gate = jnp.sum(probs * onehot, axis=1, keepdims=True)
    extra_ref[:, 0:experts] = (onehot - probs).astype(BF16)
    extra_ref[:, experts:] = jnp.zeros((n_tok, EXTRA - experts), BF16)
    copies[2].wait()
    rhs_ref[pl.ds(n_tok, n_tok), :] = (gate * og_ref[...].astype(F32)).astype(BF16)
    copies[3].wait()
    copies[4].wait()
    router = rw_ref[...].astype(F32)
    place = iota((2 * CAP, EXTRA), 0)
    pieces = jnp.zeros((2 * CAP, EXTRA), F32)
    for k in range(width // EXTRA):
        piece = jnp.broadcast_to(router[:, k * EXTRA : (k + 1) * EXTRA], (2 * CAP, EXTRA))
        pieces = jnp.where(place == k, piece, pieces)
    part = rows // 4
    outs = []
    for start in range(0, rows, part):
        row = iota((part, n_tok), 0) + start
        first = jnp.where(row == slot, 1.0, 0.0).astype(BF16)
        second = jnp.where(row == slot + CAP, 1.0, 0.0).astype(BF16)
        both = jnp.concatenate([first, second], axis=1)
        send_ref[start : start + part, 0:width] = dot(both, rhs_ref[...]).astype(BF16)
        side = dot(second, extra_ref[...]).reshape(part // (2 * CAP), 2 * CAP, EXTRA)
        side = side + pieces[None]
        send_ref[start : start + part, width:] = side.reshape(part, EXTRA).astype(BF16)
        out = pltpu.make_async_copy(
            send_ref.at[pl.ds(start, part), :],
            send_hbm.at[pl.ds(start, part), :],
            out_sems.at[start // part],
        )
        out.start()
        outs.append(out)
    for out in outs:
        out.wait()


def prep(ids, logits, tokens, out_grad, router_weight):
    n_tok, width = tokens.shape
    experts = logits.shape[1]
    rows = experts * 2 * CAP
    return pl.pallas_call(
        prep_kernel,
        out_shape=(
            jax.ShapeDtypeStruct((rows, width + EXTRA), BF16),
            jax.ShapeDtypeStruct((1, n_tok), jnp.int32),
        ),
        in_specs=[pl.BlockSpec(memory_space=pltpu.HBM)] * 5,
        out_specs=(
            pl.BlockSpec(memory_space=pltpu.HBM),
            pl.BlockSpec(memory_space=pltpu.VMEM),
        ),
        scratch_shapes=[
            pltpu.VMEM((1, n_tok), jnp.int32),
            pltpu.VMEM((n_tok, experts), F32),
            pltpu.VMEM((2 * n_tok, width), BF16),
            pltpu.VMEM((n_tok, width), BF16),
            pltpu.VMEM((1, width), BF16),
            pltpu.VMEM((n_tok, EXTRA), BF16),
            pltpu.VMEM((rows, width + EXTRA), BF16),
            pltpu.SemaphoreType.DMA((5,)),
            pltpu.SemaphoreType.DMA((4,)),
        ],
        compiler_params=pltpu.CompilerParams(vmem_limit_bytes=PREP_VMEM),
    )(ids, logits, tokens, out_grad, router_weight)


def split_halves(block):
    rows, columns = block.shape
    tiles = block.astype(F32).reshape(rows // 16, 2, 8, columns)
    even, odd = tiles[:, 0], tiles[:, 1]
    low = iota(even.shape, 1) < 4
    first = jnp.where(low, even, pltpu.roll(odd, 4, axis=1))
    second = jnp.where(low, pltpu.roll(even, 4, axis=1), odd)
    return first.reshape(rows // 2, columns).astype(BF16), second.reshape(rows // 2, columns).astype(BF16)


def join_halves(first, second):
    rows, columns = first.shape
    a = first.reshape(rows // 8, 8, columns)
    b = second.reshape(rows // 8, 8, columns)
    low = iota(a.shape, 1) < 4
    even = jnp.where(low, a, pltpu.roll(b, 4, axis=1))
    odd = jnp.where(low, pltpu.roll(a, 4, axis=1), b)
    return jnp.stack([even, odd], axis=1).reshape(2 * rows, columns)


def expert_kernel(
    recv_ref, w_in_hbm, w_out_hbm, back_hbm, routed_hbm, scaled_hbm, hidden_hbm, hgrad_hbm,
    w_in_ref, w_out_ref, back_ref, routed_ref, scaled_ref, hidden_ref, hgrad_ref, part_ref,
    in_sems, out_sems,
):
    rows = routed_ref.shape[0]
    width, inner = w_in_ref.shape
    experts = rows // CAP
    half = width // 2
    block = inner // BLOCKS
    loads = []
    for i in range(BLOCKS):
        cut = pl.ds(i * block, block)
        loads.append(
            (
                pltpu.make_async_copy(w_in_hbm.at[0, :, cut], w_in_ref.at[:, cut], in_sems.at[0, i]),
                pltpu.make_async_copy(w_out_hbm.at[0, cut, :], w_out_ref.at[cut, :], in_sems.at[1, i]),
            )
        )
    for pair in loads:
        for load in pair:
            load.start()
    stores = []

    def store(src, dst):
        copy = pltpu.make_async_copy(src, dst, out_sems.at[len(stores)])
        copy.start()
        stores.append(copy)

    for k in range(0, width + EXTRA, 256):
        first, second = split_halves(recv_ref[:, k : k + 256])
        routed_ref[:, k : k + 256] = first
        scaled_ref[:, k : k + 256] = second
    store(routed_ref.at[:, pl.ds(0, width)], routed_hbm)
    store(scaled_ref.at[:, pl.ds(0, width)], scaled_hbm)
    c = jnp.zeros((rows, 1), F32)
    for i in range(BLOCKS):
        k = i * block
        loads[i][0].wait()
        pre = dot(routed_ref[:, 0:width], w_in_ref[:, k : k + block])
        loads[i][1].wait()
        back = dot(scaled_ref[:, 0:width], w_out_ref[k : k + block, :], 1, 1)
        hidden = jnp.maximum(pre, 0.0)
        hidden_ref[:, k : k + block] = hidden.astype(BF16)
        hgrad_ref[:, k : k + block] = jnp.where(pre > 0.0, back, 0.0).astype(BF16)
        c = c + jnp.sum(hidden * back, axis=1, keepdims=True)
        cut = pl.ds(k, block)
        store(hidden_ref.at[:, cut], hidden_hbm.at[:, cut])
        store(hgrad_ref.at[:, cut], hgrad_hbm.at[:, cut])
    q = scaled_ref[:, width : width + experts].astype(F32)
    logit_grad = (c * q).astype(BF16)
    part = dot(logit_grad, routed_ref[:, 0:width], 0, 0)
    for k in range(width // 128):
        part_ref[pl.ds(k, experts, stride=8), :] = part[:, k * 128 : (k + 1) * 128]
    back_ref[:, half:] = part_ref[...].astype(BF16)
    store(back_ref.at[:, pl.ds(half, 128)], back_hbm.at[:, pl.ds(half, 128)])
    pieces = routed_ref[:, width : width + EXTRA]

    def grad_piece(k):
        pick = jnp.where(iota((experts, rows), 1) == iota((experts, rows), 0) * CAP + k, 1.0, 0.0)
        router = dot(pick.astype(BF16), pieces).astype(BF16)
        grad = dot(hgrad_ref[...], w_in_ref[k * EXTRA : (k + 1) * EXTRA, :], 1, 1)
        return grad + dot(logit_grad, router)

    for k in range(half // EXTRA):
        joined = join_halves(grad_piece(k), grad_piece(half // EXTRA + k))
        back_ref[:, k * EXTRA : (k + 1) * EXTRA] = joined.astype(BF16)
        cut = pl.ds(k * EXTRA, EXTRA)
        store(back_ref.at[:, cut], back_hbm.at[:, cut])
    for copy in stores:
        copy.wait()


def expert(recv, w_in, w_out):
    rows2, columns = recv.shape
    rows = rows2 // 2
    width, inner = w_in.shape[1:]
    experts = rows // CAP
    shapes = [(rows2, width // 2 + 128), (rows, width), (rows, width), (rows, inner), (rows, inner)]
    return pl.pallas_call(
        expert_kernel,
        out_shape=tuple(jax.ShapeDtypeStruct(shape, BF16) for shape in shapes),
        in_specs=[
            pl.BlockSpec(memory_space=pltpu.VMEM),
            pl.BlockSpec(memory_space=pltpu.HBM),
            pl.BlockSpec(memory_space=pltpu.HBM),
        ],
        out_specs=(pl.BlockSpec(memory_space=pltpu.HBM),) * 5,
        scratch_shapes=[
            pltpu.VMEM((width, inner), BF16),
            pltpu.VMEM((inner, width), BF16),
            pltpu.VMEM(shapes[0], BF16),
            pltpu.VMEM((rows, columns), BF16),
            pltpu.VMEM((rows, columns), BF16),
            pltpu.VMEM((rows, inner), BF16),
            pltpu.VMEM((rows, inner), BF16),
            pltpu.VMEM((experts * 8, 128), F32),
            pltpu.SemaphoreType.DMA((2, BLOCKS)),
            pltpu.SemaphoreType.DMA((2 * BLOCKS + 5,)),
        ],
        compiler_params=pltpu.CompilerParams(vmem_limit_bytes=EXPERT_VMEM),
    )(recv, w_in, w_out)


def weight_kernel(routed_ref, scaled_ref, hidden_ref, hgrad_ref, d_in_ref, d_out_ref):
    width = d_in_ref.shape[0]
    d_in_ref[...] = dot(routed_ref[:, 0:width], hgrad_ref[...], 0, 0).astype(BF16)
    d_out_ref[...] = dot(hidden_ref[...], scaled_ref[:, 0:width], 0, 0).astype(BF16)


def weight_grads(routed, scaled, hidden, hgrad, width):
    rows, inner = hidden.shape
    block = 512
    whole = lambda i: (0, 0)
    flops = 2 * 2 * rows * inner * width
    moved = 2 * (2 * rows * inner + 2 * rows * width + 2 * inner * width)
    return pl.pallas_call(
        weight_kernel,
        grid=(inner // block,),
        out_shape=(
            jax.ShapeDtypeStruct((width, inner), BF16),
            jax.ShapeDtypeStruct((inner, width), BF16),
        ),
        in_specs=[
            pl.BlockSpec(routed.shape, whole),
            pl.BlockSpec(scaled.shape, whole),
            pl.BlockSpec((rows, block), lambda i: (0, i)),
            pl.BlockSpec((rows, block), lambda i: (0, i)),
        ],
        out_specs=(
            pl.BlockSpec((width, block), lambda i: (0, i)),
            pl.BlockSpec((block, width), lambda i: (i, 0)),
        ),
        compiler_params=pltpu.CompilerParams(vmem_limit_bytes=VMEM_LIMIT),
        cost_estimate=pl.CostEstimate(flops=flops, bytes_accessed=moved, transcendentals=0),
    )(routed, scaled, hidden, hgrad)


def post_kernel(recv_ref, slot_ref, d_tok_ref, d_router_ref):
    rows = recv_ref.shape[0]
    n_tok, width = d_tok_ref.shape
    half = width // 2
    row = iota((rows, n_tok), 0)
    slot = slot_ref[...]
    first = jnp.where(row == slot, 1.0, 0.0).astype(BF16)
    second = jnp.where(row == slot + CAP, 1.0, 0.0).astype(BF16)
    d_tok_ref[:, 0:half] = dot(first, recv_ref[:, 0:half], 0, 0).astype(BF16)
    d_tok_ref[:, half:] = dot(second, recv_ref[:, 0:half], 0, 0).astype(BF16)
    parts = recv_ref[:, half:].astype(F32).reshape(rows // 8, 8, 128)
    total = jnp.sum(parts, axis=0)
    for k in range(width // 128):
        d_router_ref[:, k * 128 : (k + 1) * 128] = total[k : k + 1, :]


def post(recv, slot, n_tok, width):
    return pl.pallas_call(
        post_kernel,
        out_shape=(
            jax.ShapeDtypeStruct((n_tok, width), BF16),
            jax.ShapeDtypeStruct((1, width), F32),
        ),
        compiler_params=pltpu.CompilerParams(vmem_limit_bytes=VMEM_LIMIT),
    )(recv, slot)


def exchange(rows, experts):
    count, columns = rows.shape
    cut = rows.reshape(experts, count // experts, columns)
    return lax.all_to_all(cut, AXES, split_axis=0, concat_axis=0, tiled=True).reshape(count, columns)


def per_device(tokens, out_grad, expert_ids, router_logits, router_weight, w_in, w_out):
    experts = router_logits.shape[1]
    n_tok, width = tokens.shape
    send, slot = prep(expert_ids.reshape(1, n_tok), router_logits, tokens, out_grad, router_weight)
    recv = exchange(send, experts)
    ret, routed, scaled, hidden, hgrad = expert(recv, w_in, w_out)
    got = exchange(ret, experts)
    d_in, d_out = weight_grads(routed, scaled, hidden, hgrad, width)
    d_tokens, d_router = post(got, slot, n_tok, width)
    return (d_tokens, d_in[None], d_out[None], d_router)


def solution(mesh):
    rows = P(AXES, None)
    cube = P(AXES, None, None)
    return jax.shard_map(
        per_device,
        mesh=mesh,
        in_specs=(rows, rows, P(AXES), rows, rows, cube, cube),
        out_specs=(rows, cube, cube, rows),
        check_vma=False,
    )
```

```python
import jax
import jax.numpy as jnp
from jax import lax
from jax.experimental import pallas as pl
from jax.experimental.pallas import tpu as pltpu
from jax.sharding import PartitionSpec as P

BF16 = jnp.bfloat16
F32 = jnp.float32
AXES = ("row", "col")
CAP = 4
EXTRA = 256
MIB = 1024 * 1024
PREP_VMEM = 63 * MIB
EXPERT_VMEM = 46 * MIB
WEIGHT_VMEM = 50 * MIB
POST_VMEM = 16 * MIB
EXPERT_BLOCKS = 1
BLOCKS = 4


def dot(a, b, ca=1, cb=0):
    return lax.dot_general(a, b, (((ca,), (cb,)), ((), ())), preferred_element_type=F32)


def iota(shape, axis):
    return lax.broadcasted_iota(jnp.int32, shape, axis)


def prep_kernel(
    ids_hbm, logits_hbm, tok_hbm, og_hbm, rw_hbm, send_hbm, slot_ref,
    ids_ref, logits_ref, rhs_ref, og_ref, rw_ref, extra_ref, send_ref, sems, out_sems,
):
    n_tok, width = og_ref.shape
    experts = logits_ref.shape[1]
    rows = send_ref.shape[0]
    copies = [
        pltpu.make_async_copy(src, dst, sems.at[i])
        for i, (src, dst) in enumerate(
            [
                (ids_hbm, ids_ref),
                (logits_hbm, logits_ref),
                (og_hbm, og_ref),
                (tok_hbm, rhs_ref.at[pl.ds(0, n_tok), :]),
                (rw_hbm, rw_ref),
            ]
        )
    ]
    for copy in copies:
        copy.start()
    upper = jnp.where(iota((n_tok, n_tok), 0) < iota((n_tok, n_tok), 1), 1.0, 0.0).astype(BF16)
    copies[0].wait()
    ids = ids_ref[...]
    onehot_t = jnp.where(iota((experts, n_tok), 0) == ids, 1.0, 0.0).astype(F32)
    earlier = dot(onehot_t.astype(BF16), upper)
    rank = jnp.sum(earlier * onehot_t, axis=0, keepdims=True)
    slot = ids * (2 * CAP) + rank.astype(jnp.int32)
    slot_ref[...] = slot
    onehot = onehot_t.T
    copies[1].wait()
    logits = logits_ref[...]
    grown = jnp.exp(logits - jnp.max(logits, axis=1, keepdims=True))
    probs = grown / jnp.sum(grown, axis=1, keepdims=True)
    gate = jnp.sum(probs * onehot, axis=1, keepdims=True)
    extra_ref[:, 0:experts] = (onehot - probs).astype(BF16)
    extra_ref[:, experts:] = jnp.zeros((n_tok, EXTRA - experts), BF16)
    copies[2].wait()
    rhs_ref[pl.ds(n_tok, n_tok), :] = (gate * og_ref[...].astype(F32)).astype(BF16)
    copies[3].wait()
    copies[4].wait()
    router = rw_ref[...].astype(F32)
    place = iota((2 * CAP, EXTRA), 0)
    pieces = jnp.zeros((2 * CAP, EXTRA), F32)
    for k in range(width // EXTRA):
        piece = jnp.broadcast_to(router[:, k * EXTRA : (k + 1) * EXTRA], (2 * CAP, EXTRA))
        pieces = jnp.where(place == k, piece, pieces)
    part = rows // 4
    outs = []
    for start in range(0, rows, part):
        row = iota((part, n_tok), 0) + start
        first = jnp.where(row == slot, 1.0, 0.0).astype(BF16)
        second = jnp.where(row == slot + CAP, 1.0, 0.0).astype(BF16)
        both = jnp.concatenate([first, second], axis=1)
        send_ref[start : start + part, 0:width] = dot(both, rhs_ref[...]).astype(BF16)
        side = dot(second, extra_ref[...]).reshape(part // (2 * CAP), 2 * CAP, EXTRA)
        side = side + pieces[None]
        send_ref[start : start + part, width:] = side.reshape(part, EXTRA).astype(BF16)
        out = pltpu.make_async_copy(
            send_ref.at[pl.ds(start, part), :],
            send_hbm.at[pl.ds(start, part), :],
            out_sems.at[start // part],
        )
        out.start()
        outs.append(out)
    for out in outs:
        out.wait()


def prep(ids, logits, tokens, out_grad, router_weight):
    n_tok, width = tokens.shape
    experts = logits.shape[1]
    rows = experts * 2 * CAP
    return pl.pallas_call(
        prep_kernel,
        out_shape=(
            jax.ShapeDtypeStruct((rows, width + EXTRA), BF16),
            jax.ShapeDtypeStruct((1, n_tok), jnp.int32),
        ),
        in_specs=[pl.BlockSpec(memory_space=pltpu.HBM)] * 5,
        out_specs=(
            pl.BlockSpec(memory_space=pltpu.HBM),
            pl.BlockSpec(memory_space=pltpu.VMEM),
        ),
        scratch_shapes=[
            pltpu.VMEM((1, n_tok), jnp.int32),
            pltpu.VMEM((n_tok, experts), F32),
            pltpu.VMEM((2 * n_tok, width), BF16),
            pltpu.VMEM((n_tok, width), BF16),
            pltpu.VMEM((1, width), BF16),
            pltpu.VMEM((n_tok, EXTRA), BF16),
            pltpu.VMEM((rows, width + EXTRA), BF16),
            pltpu.SemaphoreType.DMA((5,)),
            pltpu.SemaphoreType.DMA((4,)),
        ],
        compiler_params=pltpu.CompilerParams(vmem_limit_bytes=PREP_VMEM),
    )(ids, logits, tokens, out_grad, router_weight)


def split_halves(block):
    rows, columns = block.shape
    tiles = block.astype(F32).reshape(rows // 16, 2, 8, columns)
    even, odd = tiles[:, 0], tiles[:, 1]
    low = iota(even.shape, 1) < 4
    first = jnp.where(low, even, pltpu.roll(odd, 4, axis=1))
    second = jnp.where(low, pltpu.roll(even, 4, axis=1), odd)
    return first.reshape(rows // 2, columns).astype(BF16), second.reshape(rows // 2, columns).astype(BF16)


def join_halves(first, second):
    rows, columns = first.shape
    a = first.reshape(rows // 8, 8, columns)
    b = second.reshape(rows // 8, 8, columns)
    low = iota(a.shape, 1) < 4
    even = jnp.where(low, a, pltpu.roll(b, 4, axis=1))
    odd = jnp.where(low, pltpu.roll(a, 4, axis=1), b)
    return jnp.stack([even, odd], axis=1).reshape(2 * rows, columns)


def expert_kernel(
    recv_ref, w_in_ref, w_out_hbm, back_hbm,
    w_out_ref, routed_ref, scaled_ref, side_ref, hgrad_ref, back_ref, part_ref, load_sems, sems,
):
    rows, width = scaled_ref.shape
    inner = hgrad_ref.shape[1]
    experts = rows // CAP
    half = width // 2
    block = inner // EXPERT_BLOCKS
    loads = []
    for i in range(EXPERT_BLOCKS):
        cut = pl.ds(i * block, block)
        load = pltpu.make_async_copy(w_out_hbm.at[0, cut, :], w_out_ref.at[cut, :], load_sems.at[i])
        load.start()
        loads.append(load)
    stores = []

    def store(start, size):
        cut = pl.ds(start, size)
        copy = pltpu.make_async_copy(back_ref.at[:, cut], back_hbm.at[:, cut], sems.at[len(stores)])
        copy.start()
        stores.append(copy)

    for k in range(0, width, EXTRA):
        first, second = split_halves(recv_ref[:, k : k + EXTRA])
        routed_ref[:, k : k + EXTRA] = first
        scaled_ref[:, k : k + EXTRA] = second
    pieces, q = split_halves(recv_ref[:, width:])
    for i in range(EXTRA // 128):
        side_ref[i] = pieces[:, i * 128 : (i + 1) * 128].astype(F32)
    q = q[:, 0:experts].astype(F32)
    c = jnp.zeros((rows, 128), F32)
    for i in range(EXPERT_BLOCKS):
        k = i * block
        pre = dot(routed_ref[...], w_in_ref[0, :, k : k + block])
        loads[i].wait()
        back = dot(scaled_ref[...], w_out_ref[k : k + block, :], 1, 1)
        hgrad = jnp.where(pre > 0.0, back, 0.0)
        hgrad_ref[:, k : k + block] = hgrad.astype(BF16)
        product = pre * hgrad
        for j in range(0, block, 128):
            c = c + product[:, j : j + 128]
    logit_grad = (jnp.sum(c, axis=1, keepdims=True) * q).astype(BF16)
    part = dot(logit_grad, routed_ref[...], 0, 0)
    for k in range(width // 128):
        part_ref[pl.ds(k, experts, stride=8), :] = part[:, k * 128 : (k + 1) * 128]
    back_ref[:, half:] = part_ref[...].astype(BF16)
    store(half, 128)

    def grad_piece(k):
        strips = [side_ref[i, pl.ds(k, experts, stride=CAP), :] for i in range(EXTRA // 128)]
        router = jnp.concatenate(strips, axis=1).astype(BF16)
        grad = dot(hgrad_ref[...], w_in_ref[0, k * EXTRA : (k + 1) * EXTRA, :], 1, 1)
        return grad + dot(logit_grad, router)

    for k in range(half // EXTRA):
        joined = join_halves(grad_piece(k), grad_piece(half // EXTRA + k))
        back_ref[:, k * EXTRA : (k + 1) * EXTRA] = joined.astype(BF16)
        store(k * EXTRA, EXTRA)
    for copy in stores:
        copy.wait()


def expert(recv, w_in, w_out):
    rows2, columns = recv.shape
    rows = rows2 // 2
    width, inner = w_in.shape[1:]
    experts = rows // CAP
    back_shape = (rows2, width // 2 + 128)
    return pl.pallas_call(
        expert_kernel,
        out_shape=jax.ShapeDtypeStruct(back_shape, BF16),
        in_specs=[
            pl.BlockSpec(memory_space=pltpu.VMEM),
            pl.BlockSpec(memory_space=pltpu.VMEM),
            pl.BlockSpec(memory_space=pltpu.HBM),
        ],
        out_specs=pl.BlockSpec(memory_space=pltpu.HBM),
        scratch_shapes=[
            pltpu.VMEM((inner, width), BF16),
            pltpu.VMEM((rows, width), BF16),
            pltpu.VMEM((rows, width), BF16),
            pltpu.VMEM((EXTRA // 128, rows, 128), F32),
            pltpu.VMEM((rows, inner), BF16),
            pltpu.VMEM(back_shape, BF16),
            pltpu.VMEM((experts * 8, 128), F32),
            pltpu.SemaphoreType.DMA((EXPERT_BLOCKS,)),
            pltpu.SemaphoreType.DMA((width // 2 // EXTRA + 1,)),
        ],
        compiler_params=pltpu.CompilerParams(vmem_limit_bytes=EXPERT_VMEM),
    )(recv, w_in, w_out)


def weight_kernel(recv_ref, w_in_ref, w_out_ref, d_in_ref, d_out_ref, routed_ref, scaled_ref):
    width = routed_ref.shape[1]

    @pl.when(pl.program_id(0) == 0)
    def _():
        for k in range(0, width, EXTRA):
            first, second = split_halves(recv_ref[:, k : k + EXTRA])
            routed_ref[:, k : k + EXTRA] = first
            scaled_ref[:, k : k + EXTRA] = second

    pre = dot(routed_ref[...], w_in_ref[0])
    back = dot(scaled_ref[...], w_out_ref[0], 1, 1)
    hidden = jnp.maximum(pre, 0.0).astype(BF16)
    hgrad = jnp.where(pre > 0.0, back, 0.0).astype(BF16)
    d_in_ref[0] = dot(routed_ref[...], hgrad, 0, 0).astype(BF16)
    d_out_ref[0] = dot(hidden, scaled_ref[...], 0, 0).astype(BF16)


def weight_grads(recv, w_in, w_out):
    rows2, columns = recv.shape
    rows = rows2 // 2
    width, inner = w_in.shape[1:]
    block = inner // BLOCKS
    flops = 4 * 2 * rows * inner * width
    moved = 2 * (rows2 * columns + 4 * inner * width)
    in_block = pl.BlockSpec((1, width, block), lambda i: (0, 0, i))
    out_block = pl.BlockSpec((1, block, width), lambda i: (0, i, 0))
    return pl.pallas_call(
        weight_kernel,
        grid=(BLOCKS,),
        out_shape=(
            jax.ShapeDtypeStruct(w_in.shape, BF16),
            jax.ShapeDtypeStruct(w_out.shape, BF16),
        ),
        in_specs=[pl.BlockSpec((rows2, columns), lambda i: (0, 0)), in_block, out_block],
        out_specs=(in_block, out_block),
        scratch_shapes=[
            pltpu.VMEM((rows, width), BF16),
            pltpu.VMEM((rows, width), BF16),
        ],
        compiler_params=pltpu.CompilerParams(vmem_limit_bytes=WEIGHT_VMEM),
        cost_estimate=pl.CostEstimate(flops=flops, bytes_accessed=moved, transcendentals=0),
    )(recv, w_in, w_out)


def post_kernel(recv_ref, slot_ref, d_tok_ref, d_router_ref):
    rows = recv_ref.shape[0]
    n_tok, width = d_tok_ref.shape
    half = width // 2
    row = iota((rows, n_tok), 0)
    slot = slot_ref[...]
    first = jnp.where(row == slot, 1.0, 0.0).astype(BF16)
    second = jnp.where(row == slot + CAP, 1.0, 0.0).astype(BF16)
    d_tok_ref[:, 0:half] = dot(first, recv_ref[:, 0:half], 0, 0).astype(BF16)
    d_tok_ref[:, half:] = dot(second, recv_ref[:, 0:half], 0, 0).astype(BF16)
    parts = recv_ref[:, half:].astype(F32).reshape(rows // 8, 8, 128)
    total = jnp.sum(parts, axis=0)
    for k in range(width // 128):
        d_router_ref[:, k * 128 : (k + 1) * 128] = total[k : k + 1, :]


def post(recv, slot, n_tok, width):
    return pl.pallas_call(
        post_kernel,
        out_shape=(
            jax.ShapeDtypeStruct((n_tok, width), BF16),
            jax.ShapeDtypeStruct((1, width), F32),
        ),
        compiler_params=pltpu.CompilerParams(vmem_limit_bytes=POST_VMEM),
    )(recv, slot)


def exchange(rows, experts):
    count, columns = rows.shape
    cut = rows.reshape(experts, count // experts, columns)
    return lax.all_to_all(cut, AXES, split_axis=0, concat_axis=0, tiled=True).reshape(count, columns)


def per_device(tokens, out_grad, expert_ids, router_logits, router_weight, w_in, w_out):
    experts = router_logits.shape[1]
    n_tok, width = tokens.shape
    send, slot = prep(expert_ids.reshape(1, n_tok), router_logits, tokens, out_grad, router_weight)
    recv = exchange(send, experts)
    got = exchange(expert(recv, w_in, w_out), experts)
    d_in, d_out = weight_grads(recv, w_in, w_out)
    d_tokens, d_router = post(got, slot, n_tok, width)
    return (d_tokens, d_in, d_out, d_router)


def solution(mesh):
    rows = P(AXES, None)
    cube = P(AXES, None, None)
    return jax.shard_map(
        per_device,
        mesh=mesh,
        in_specs=(rows, rows, P(AXES), rows, rows, cube, cube),
        out_specs=(rows, cube, cube, rows),
        check_vma=False,
    )
```

```python
import jax
import jax.numpy as jnp
from jax import lax
from jax.experimental import pallas as pl
from jax.experimental.pallas import tpu as pltpu
from jax.sharding import PartitionSpec as P

BF16 = jnp.bfloat16
F32 = jnp.float32
AXES = ("row", "col")
CAP = 4
EXTRA = 256
MIB = 1024 * 1024
PREP_VMEM = 63 * MIB
EXPERT_VMEM = 46 * MIB
WEIGHT_VMEM = 55 * MIB
POST_VMEM = 16 * MIB
EXPERT_BLOCKS = 2
BLOCKS = 4
PREP_PARTS = 8


def dot(a, b, ca=1, cb=0):
    return lax.dot_general(a, b, (((ca,), (cb,)), ((), ())), preferred_element_type=F32)


def iota(shape, axis):
    return lax.broadcasted_iota(jnp.int32, shape, axis)


def prep_kernel(
    ids_hbm, logits_hbm, tok_hbm, og_hbm, rw_hbm, send_hbm, slot_ref,
    ids_ref, logits_ref, rhs_ref, og_ref, rw_ref, extra_ref, send_ref, sems, out_sems,
):
    n_tok, width = og_ref.shape
    experts = logits_ref.shape[1]
    rows = send_ref.shape[0]
    copies = [
        pltpu.make_async_copy(src, dst, sems.at[i])
        for i, (src, dst) in enumerate(
            [
                (ids_hbm, ids_ref),
                (logits_hbm, logits_ref),
                (og_hbm, og_ref),
                (tok_hbm, rhs_ref.at[pl.ds(0, n_tok), :]),
                (rw_hbm, rw_ref),
            ]
        )
    ]
    for copy in copies:
        copy.start()
    upper = jnp.where(iota((n_tok, n_tok), 0) < iota((n_tok, n_tok), 1), 1.0, 0.0).astype(BF16)
    copies[0].wait()
    ids = ids_ref[...]
    onehot_t = jnp.where(iota((experts, n_tok), 0) == ids, 1.0, 0.0).astype(F32)
    earlier = dot(onehot_t.astype(BF16), upper)
    rank = jnp.sum(earlier * onehot_t, axis=0, keepdims=True)
    slot = ids * (2 * CAP) + rank.astype(jnp.int32)
    slot_ref[...] = slot
    onehot = onehot_t.T
    copies[1].wait()
    logits = logits_ref[...]
    grown = jnp.exp(logits - jnp.max(logits, axis=1, keepdims=True))
    probs = grown / jnp.sum(grown, axis=1, keepdims=True)
    gate = jnp.sum(probs * onehot, axis=1, keepdims=True)
    extra_ref[:, 0:experts] = (onehot - probs).astype(BF16)
    extra_ref[:, experts:] = jnp.zeros((n_tok, EXTRA - experts), BF16)
    copies[2].wait()
    rhs_ref[pl.ds(n_tok, n_tok), :] = (gate * og_ref[...].astype(F32)).astype(BF16)
    copies[3].wait()
    copies[4].wait()
    router = rw_ref[...].astype(F32)
    place = iota((2 * CAP, EXTRA), 0)
    pieces = jnp.zeros((2 * CAP, EXTRA), F32)
    for k in range(width // EXTRA):
        piece = jnp.broadcast_to(router[:, k * EXTRA : (k + 1) * EXTRA], (2 * CAP, EXTRA))
        pieces = jnp.where(place == k, piece, pieces)
    part = rows // PREP_PARTS
    outs = []
    for start in range(0, rows, part):
        row = iota((part, n_tok), 0) + start
        first = jnp.where(row == slot, 1.0, 0.0).astype(BF16)
        second = jnp.where(row == slot + CAP, 1.0, 0.0).astype(BF16)
        both = jnp.concatenate([first, second], axis=1)
        send_ref[start : start + part, 0:width] = dot(both, rhs_ref[...]).astype(BF16)
        side = dot(second, extra_ref[...]).reshape(part // (2 * CAP), 2 * CAP, EXTRA)
        side = side + pieces[None]
        send_ref[start : start + part, width:] = side.reshape(part, EXTRA).astype(BF16)
        out = pltpu.make_async_copy(
            send_ref.at[pl.ds(start, part), :],
            send_hbm.at[pl.ds(start, part), :],
            out_sems.at[start // part],
        )
        out.start()
        outs.append(out)
    for out in outs:
        out.wait()


def prep(ids, logits, tokens, out_grad, router_weight):
    n_tok, width = tokens.shape
    experts = logits.shape[1]
    rows = experts * 2 * CAP
    return pl.pallas_call(
        prep_kernel,
        out_shape=(
            jax.ShapeDtypeStruct((rows, width + EXTRA), BF16),
            jax.ShapeDtypeStruct((1, n_tok), jnp.int32),
        ),
        in_specs=[pl.BlockSpec(memory_space=pltpu.HBM)] * 5,
        out_specs=(
            pl.BlockSpec(memory_space=pltpu.HBM),
            pl.BlockSpec(memory_space=pltpu.VMEM),
        ),
        scratch_shapes=[
            pltpu.VMEM((1, n_tok), jnp.int32),
            pltpu.VMEM((n_tok, experts), F32),
            pltpu.VMEM((2 * n_tok, width), BF16),
            pltpu.VMEM((n_tok, width), BF16),
            pltpu.VMEM((1, width), BF16),
            pltpu.VMEM((n_tok, EXTRA), BF16),
            pltpu.VMEM((rows, width + EXTRA), BF16),
            pltpu.SemaphoreType.DMA((5,)),
            pltpu.SemaphoreType.DMA((PREP_PARTS,)),
        ],
        compiler_params=pltpu.CompilerParams(vmem_limit_bytes=PREP_VMEM),
    )(ids, logits, tokens, out_grad, router_weight)


def split_halves(block):
    rows, columns = block.shape
    tiles = block.astype(F32).reshape(rows // 16, 2, 8, columns)
    even, odd = tiles[:, 0], tiles[:, 1]
    low = iota(even.shape, 1) < 4
    first = jnp.where(low, even, pltpu.roll(odd, 4, axis=1))
    second = jnp.where(low, pltpu.roll(even, 4, axis=1), odd)
    return first.reshape(rows // 2, columns).astype(BF16), second.reshape(rows // 2, columns).astype(BF16)


def join_halves(first, second):
    rows, columns = first.shape
    a = first.reshape(rows // 8, 8, columns)
    b = second.reshape(rows // 8, 8, columns)
    low = iota(a.shape, 1) < 4
    even = jnp.where(low, a, pltpu.roll(b, 4, axis=1))
    odd = jnp.where(low, pltpu.roll(a, 4, axis=1), b)
    return jnp.stack([even, odd], axis=1).reshape(2 * rows, columns)


def expert_kernel(
    recv_ref, w_in_ref, w_out_hbm, back_hbm,
    w_out_ref, routed_ref, scaled_ref, side_ref, hgrad_ref, back_ref, part_ref, load_sems, sems,
):
    rows, width = scaled_ref.shape
    inner = hgrad_ref.shape[1]
    experts = rows // CAP
    half = width // 2
    block = inner // EXPERT_BLOCKS
    loads = []
    for i in range(EXPERT_BLOCKS):
        cut = pl.ds(i * block, block)
        load = pltpu.make_async_copy(w_out_hbm.at[0, cut, :], w_out_ref.at[cut, :], load_sems.at[i])
        load.start()
        loads.append(load)
    stores = []

    def store(start, size):
        cut = pl.ds(start, size)
        copy = pltpu.make_async_copy(back_ref.at[:, cut], back_hbm.at[:, cut], sems.at[len(stores)])
        copy.start()
        stores.append(copy)

    for k in range(0, width, EXTRA):
        first, second = split_halves(recv_ref[:, k : k + EXTRA])
        routed_ref[:, k : k + EXTRA] = first
        scaled_ref[:, k : k + EXTRA] = second
    pieces, q = split_halves(recv_ref[:, width:])
    for i in range(EXTRA // 128):
        side_ref[i] = pieces[:, i * 128 : (i + 1) * 128].astype(F32)
    q = q[:, 0:experts].astype(F32)
    c = jnp.zeros((rows, 128), F32)
    pre_all = dot(routed_ref[...], w_in_ref[0])
    for i in range(EXPERT_BLOCKS):
        k = i * block
        pre = pre_all[:, k : k + block]
        loads[i].wait()
        back = dot(scaled_ref[...], w_out_ref[k : k + block, :], 1, 1)
        hgrad = jnp.where(pre > 0.0, back, 0.0)
        hgrad_ref[:, k : k + block] = hgrad.astype(BF16)
        product = pre * hgrad
        for j in range(0, block, 128):
            c = c + product[:, j : j + 128]
    logit_grad = (jnp.sum(c, axis=1, keepdims=True) * q).astype(BF16)
    part = dot(logit_grad, routed_ref[...], 0, 0)
    for k in range(width // 128):
        part_ref[pl.ds(k, experts, stride=8), :] = part[:, k * 128 : (k + 1) * 128]
    back_ref[:, half:] = part_ref[...].astype(BF16)
    store(half, 128)

    def grad_piece(k):
        strips = [side_ref[i, pl.ds(k, experts, stride=CAP), :] for i in range(EXTRA // 128)]
        router = jnp.concatenate(strips, axis=1).astype(BF16)
        grad = dot(hgrad_ref[...], w_in_ref[0, k * EXTRA : (k + 1) * EXTRA, :], 1, 1)
        return grad + dot(logit_grad, router)

    for k in range(half // EXTRA):
        joined = join_halves(grad_piece(k), grad_piece(half // EXTRA + k))
        back_ref[:, k * EXTRA : (k + 1) * EXTRA] = joined.astype(BF16)
        store(k * EXTRA, EXTRA)
    for copy in stores:
        copy.wait()


def expert(recv, w_in, w_out):
    rows2, columns = recv.shape
    rows = rows2 // 2
    width, inner = w_in.shape[1:]
    experts = rows // CAP
    back_shape = (rows2, width // 2 + 128)
    return pl.pallas_call(
        expert_kernel,
        out_shape=jax.ShapeDtypeStruct(back_shape, BF16),
        in_specs=[
            pl.BlockSpec(memory_space=pltpu.VMEM),
            pl.BlockSpec(memory_space=pltpu.VMEM),
            pl.BlockSpec(memory_space=pltpu.HBM),
        ],
        out_specs=pl.BlockSpec(memory_space=pltpu.HBM),
        scratch_shapes=[
            pltpu.VMEM((inner, width), BF16),
            pltpu.VMEM((rows, width), BF16),
            pltpu.VMEM((rows, width), BF16),
            pltpu.VMEM((EXTRA // 128, rows, 128), F32),
            pltpu.VMEM((rows, inner), BF16),
            pltpu.VMEM(back_shape, BF16),
            pltpu.VMEM((experts * 8, 128), F32),
            pltpu.SemaphoreType.DMA((EXPERT_BLOCKS,)),
            pltpu.SemaphoreType.DMA((width // 2 // EXTRA + 1,)),
        ],
        compiler_params=pltpu.CompilerParams(vmem_limit_bytes=EXPERT_VMEM),
    )(recv, w_in, w_out)


def weight_kernel(recv_ref, w_in_ref, w_out_ref, d_in_ref, d_out_ref, routed_ref, scaled_ref):
    width = routed_ref.shape[1]

    @pl.when(pl.program_id(0) == 0)
    def _():
        for k in range(0, width, EXTRA):
            first, second = split_halves(recv_ref[:, k : k + EXTRA])
            routed_ref[:, k : k + EXTRA] = first
            scaled_ref[:, k : k + EXTRA] = second

    pre = dot(routed_ref[...], w_in_ref[0])
    back = dot(scaled_ref[...], w_out_ref[0], 1, 1)
    hidden = jnp.maximum(pre, 0.0).astype(BF16)
    hgrad = jnp.where(pre > 0.0, back, 0.0).astype(BF16)
    d_in_ref[0] = dot(routed_ref[...], hgrad, 0, 0).astype(BF16)
    d_out_ref[0] = dot(hidden, scaled_ref[...], 0, 0).astype(BF16)


def weight_grads(recv, w_in, w_out):
    rows2, columns = recv.shape
    rows = rows2 // 2
    width, inner = w_in.shape[1:]
    block = inner // BLOCKS
    flops = 4 * 2 * rows * inner * width
    moved = 2 * (rows2 * columns + 4 * inner * width)
    in_block = pl.BlockSpec((1, width, block), lambda i: (0, 0, i))
    out_block = pl.BlockSpec((1, block, width), lambda i: (0, i, 0))
    return pl.pallas_call(
        weight_kernel,
        grid=(BLOCKS,),
        out_shape=(
            jax.ShapeDtypeStruct(w_in.shape, BF16),
            jax.ShapeDtypeStruct(w_out.shape, BF16),
        ),
        in_specs=[pl.BlockSpec((rows2, columns), lambda i: (0, 0)), in_block, out_block],
        out_specs=(in_block, out_block),
        scratch_shapes=[
            pltpu.VMEM((rows, width), BF16),
            pltpu.VMEM((rows, width), BF16),
        ],
        compiler_params=pltpu.CompilerParams(vmem_limit_bytes=WEIGHT_VMEM),
        cost_estimate=pl.CostEstimate(flops=flops, bytes_accessed=moved, transcendentals=0),
    )(recv, w_in, w_out)


def post_kernel(recv_ref, slot_ref, d_tok_ref, d_router_ref):
    rows = recv_ref.shape[0]
    n_tok, width = d_tok_ref.shape
    half = width // 2
    row = iota((rows, n_tok), 0)
    slot = slot_ref[...]
    first = jnp.where(row == slot, 1.0, 0.0).astype(BF16)
    second = jnp.where(row == slot + CAP, 1.0, 0.0).astype(BF16)
    d_tok_ref[:, 0:half] = dot(first, recv_ref[:, 0:half], 0, 0).astype(BF16)
    d_tok_ref[:, half:] = dot(second, recv_ref[:, 0:half], 0, 0).astype(BF16)
    parts = recv_ref[:, half:].astype(F32).reshape(rows // 8, 8, 128)
    total = jnp.sum(parts, axis=0)
    for k in range(width // 128):
        d_router_ref[:, k * 128 : (k + 1) * 128] = total[k : k + 1, :]


def post(recv, slot, n_tok, width):
    return pl.pallas_call(
        post_kernel,
        out_shape=(
            jax.ShapeDtypeStruct((n_tok, width), BF16),
            jax.ShapeDtypeStruct((1, width), F32),
        ),
        compiler_params=pltpu.CompilerParams(vmem_limit_bytes=POST_VMEM),
    )(recv, slot)


def exchange(rows, experts):
    count, columns = rows.shape
    cut = rows.reshape(experts, count // experts, columns)
    return lax.all_to_all(cut, AXES, split_axis=0, concat_axis=0, tiled=True).reshape(count, columns)


def per_device(tokens, out_grad, expert_ids, router_logits, router_weight, w_in, w_out):
    experts = router_logits.shape[1]
    n_tok, width = tokens.shape
    send, slot = prep(expert_ids.reshape(1, n_tok), router_logits, tokens, out_grad, router_weight)
    recv = exchange(send, experts)
    got = exchange(expert(recv, w_in, w_out), experts)
    d_in, d_out = weight_grads(recv, w_in, w_out)
    d_tokens, d_router = post(got, slot, n_tok, width)
    return (d_tokens, d_in, d_out, d_router)


def solution(mesh):
    rows = P(AXES, None)
    cube = P(AXES, None, None)
    return jax.shard_map(
        per_device,
        mesh=mesh,
        in_specs=(rows, rows, P(AXES), rows, rows, cube, cube),
        out_specs=(rows, cube, cube, rows),
        check_vma=False,
    )
```

```python
import jax
import jax.numpy as jnp
from jax import lax
from jax.experimental import pallas as pl
from jax.experimental.pallas import tpu as pltpu
from jax.sharding import PartitionSpec as P

BF16 = jnp.bfloat16
F32 = jnp.float32
AXES = ("row", "col")
CAP = 4
EXTRA = 128
PIECE = 256
MIB = 1024 * 1024
PREP_VMEM = 63 * MIB
EXPERT_VMEM = 46 * MIB
WEIGHT_VMEM = 55 * MIB
POST_VMEM = 16 * MIB
EXPERT_BLOCKS = 2
BLOCKS = 4
PREP_PARTS = 8


def dot(a, b, ca=1, cb=0):
    return lax.dot_general(a, b, (((ca,), (cb,)), ((), ())), preferred_element_type=F32)


def iota(shape, axis):
    return lax.broadcasted_iota(jnp.int32, shape, axis)


def prep_kernel(
    ids_hbm, logits_hbm, tok_hbm, og_hbm, rw_hbm, send_hbm, slot_ref, q_ref,
    ids_ref, logits_ref, rhs_ref, og_ref, rw_ref, send_ref, sems, out_sems,
):
    n_tok, width = og_ref.shape
    experts = logits_ref.shape[1]
    rows = send_ref.shape[0]
    copies = [
        pltpu.make_async_copy(src, dst, sems.at[i])
        for i, (src, dst) in enumerate(
            [
                (ids_hbm, ids_ref),
                (logits_hbm, logits_ref),
                (og_hbm, og_ref),
                (tok_hbm, rhs_ref.at[pl.ds(0, n_tok), :]),
                (rw_hbm, rw_ref),
            ]
        )
    ]
    for copy in copies:
        copy.start()
    upper = jnp.where(iota((n_tok, n_tok), 0) < iota((n_tok, n_tok), 1), 1.0, 0.0).astype(BF16)
    copies[0].wait()
    ids = ids_ref[...]
    onehot_t = jnp.where(iota((experts, n_tok), 0) == ids, 1.0, 0.0).astype(F32)
    earlier = dot(onehot_t.astype(BF16), upper)
    rank = jnp.sum(earlier * onehot_t, axis=0, keepdims=True)
    slot = ids * (2 * CAP) + rank.astype(jnp.int32)
    slot_ref[...] = slot
    onehot = onehot_t.T
    copies[1].wait()
    logits = logits_ref[...]
    grown = jnp.exp(logits - jnp.max(logits, axis=1, keepdims=True))
    probs = grown / jnp.sum(grown, axis=1, keepdims=True)
    gate = jnp.sum(probs * onehot, axis=1, keepdims=True)
    q = (onehot - probs).astype(BF16)
    q_ref[...] = q
    copies[2].wait()
    rhs_ref[pl.ds(n_tok, n_tok), :] = (gate * og_ref[...].astype(F32)).astype(BF16)
    copies[3].wait()
    copies[4].wait()
    router = rw_ref[...].astype(F32)
    group = 4 * CAP
    place = iota((group, EXTRA), 0)
    pieces = jnp.zeros((group, EXTRA), F32)
    for k in range(2 * CAP):
        piece = jnp.broadcast_to(router[:, k * EXTRA : (k + 1) * EXTRA], (group, EXTRA))
        pieces = jnp.where(place == k + k // CAP * CAP, piece, pieces)
    part = rows // PREP_PARTS
    outs = []
    for start in range(0, rows, part):
        row = iota((part, n_tok), 0) + start
        first = jnp.where(row == slot, 1.0, 0.0).astype(BF16)
        second = jnp.where(row == slot + CAP, 1.0, 0.0).astype(BF16)
        both = jnp.concatenate([first, second], axis=1)
        send_ref[start : start + part, 0:width] = dot(both, rhs_ref[...]).astype(BF16)
        side = dot(second, q).reshape(part // group, group, EXTRA)
        side = side + pieces[None]
        send_ref[start : start + part, width:] = side.reshape(part, EXTRA).astype(BF16)
        out = pltpu.make_async_copy(
            send_ref.at[pl.ds(start, part), :],
            send_hbm.at[pl.ds(start, part), :],
            out_sems.at[start // part],
        )
        out.start()
        outs.append(out)
    for out in outs:
        out.wait()


def prep(ids, logits, tokens, out_grad, router_weight):
    n_tok, width = tokens.shape
    experts = logits.shape[1]
    rows = experts * 2 * CAP
    return pl.pallas_call(
        prep_kernel,
        out_shape=(
            jax.ShapeDtypeStruct((rows, width + EXTRA), BF16),
            jax.ShapeDtypeStruct((1, n_tok), jnp.int32),
            jax.ShapeDtypeStruct((n_tok, experts), BF16),
        ),
        in_specs=[pl.BlockSpec(memory_space=pltpu.HBM)] * 5,
        out_specs=(
            pl.BlockSpec(memory_space=pltpu.HBM),
            pl.BlockSpec(memory_space=pltpu.VMEM),
            pl.BlockSpec(memory_space=pltpu.VMEM),
        ),
        scratch_shapes=[
            pltpu.VMEM((1, n_tok), jnp.int32),
            pltpu.VMEM((n_tok, experts), F32),
            pltpu.VMEM((2 * n_tok, width), BF16),
            pltpu.VMEM((n_tok, width), BF16),
            pltpu.VMEM((1, width), BF16),
            pltpu.VMEM((rows, width + EXTRA), BF16),
            pltpu.SemaphoreType.DMA((5,)),
            pltpu.SemaphoreType.DMA((PREP_PARTS,)),
        ],
        compiler_params=pltpu.CompilerParams(vmem_limit_bytes=PREP_VMEM),
    )(ids, logits, tokens, out_grad, router_weight)


def split_halves(block):
    rows, columns = block.shape
    tiles = block.astype(F32).reshape(rows // 16, 2, 8, columns)
    even, odd = tiles[:, 0], tiles[:, 1]
    low = iota(even.shape, 1) < 4
    first = jnp.where(low, even, pltpu.roll(odd, 4, axis=1))
    second = jnp.where(low, pltpu.roll(even, 4, axis=1), odd)
    return first.reshape(rows // 2, columns).astype(BF16), second.reshape(rows // 2, columns).astype(BF16)


def join_halves(first, second):
    rows, columns = first.shape
    a = first.reshape(rows // 8, 8, columns)
    b = second.reshape(rows // 8, 8, columns)
    low = iota(a.shape, 1) < 4
    even = jnp.where(low, a, pltpu.roll(b, 4, axis=1))
    odd = jnp.where(low, pltpu.roll(a, 4, axis=1), b)
    return jnp.stack([even, odd], axis=1).reshape(2 * rows, columns)


def expert_kernel(
    recv_ref, w_in_ref, w_out_hbm, back_hbm, router_ref,
    w_out_ref, routed_ref, scaled_ref, side_ref, hgrad_ref, back_ref, part_ref, load_sems, sems,
):
    rows, width = scaled_ref.shape
    inner = hgrad_ref.shape[1]
    experts = rows // CAP
    half = width // 2
    block = inner // EXPERT_BLOCKS
    loads = []
    for i in range(EXPERT_BLOCKS):
        cut = pl.ds(i * block, block)
        load = pltpu.make_async_copy(w_out_hbm.at[0, cut, :], w_out_ref.at[cut, :], load_sems.at[i])
        load.start()
        loads.append(load)
    stores = []

    def store(start, size):
        cut = pl.ds(start, size)
        copy = pltpu.make_async_copy(back_ref.at[:, cut], back_hbm.at[:, cut], sems.at[len(stores)])
        copy.start()
        stores.append(copy)

    for k in range(0, width, PIECE):
        first, second = split_halves(recv_ref[:, k : k + PIECE])
        routed_ref[:, k : k + PIECE] = first
        scaled_ref[:, k : k + PIECE] = second
    pieces, q = split_halves(recv_ref[:, width:])
    side_ref[...] = pieces.astype(F32)
    for k in range(CAP):
        strip = side_ref[pl.ds(k, experts, stride=CAP), :]
        router_ref[:, k * EXTRA : (k + 1) * EXTRA] = strip.astype(BF16)
    q = q.astype(F32)
    c = jnp.zeros((rows, 128), F32)
    pre_all = dot(routed_ref[...], w_in_ref[0])
    for i in range(EXPERT_BLOCKS):
        k = i * block
        pre = pre_all[:, k : k + block]
        loads[i].wait()
        back = dot(scaled_ref[...], w_out_ref[k : k + block, :], 1, 1)
        hgrad = jnp.where(pre > 0.0, back, 0.0)
        hgrad_ref[:, k : k + block] = hgrad.astype(BF16)
        product = pre * hgrad
        for j in range(0, block, 128):
            c = c + product[:, j : j + 128]
    logit_grad = (jnp.sum(c, axis=1, keepdims=True) * q).astype(BF16)
    part = dot(logit_grad, routed_ref[...], 0, 0)
    for k in range(width // 128):
        part_ref[pl.ds(k, experts, stride=8), :] = part[:, k * 128 : (k + 1) * 128]
    back_ref[:, half:] = part_ref[...].astype(BF16)
    store(half, 128)

    def grad_piece(k):
        return dot(hgrad_ref[...], w_in_ref[0, k * PIECE : (k + 1) * PIECE, :], 1, 1)

    for k in range(half // PIECE):
        joined = join_halves(grad_piece(k), grad_piece(half // PIECE + k))
        back_ref[:, k * PIECE : (k + 1) * PIECE] = joined.astype(BF16)
        store(k * PIECE, PIECE)
    for copy in stores:
        copy.wait()


def expert(recv, w_in, w_out):
    rows2, columns = recv.shape
    rows = rows2 // 2
    width, inner = w_in.shape[1:]
    experts = rows // CAP
    back_shape = (rows2, width // 2 + 128)
    return pl.pallas_call(
        expert_kernel,
        out_shape=(
            jax.ShapeDtypeStruct(back_shape, BF16),
            jax.ShapeDtypeStruct((experts, CAP * EXTRA), BF16),
        ),
        in_specs=[
            pl.BlockSpec(memory_space=pltpu.VMEM),
            pl.BlockSpec(memory_space=pltpu.VMEM),
            pl.BlockSpec(memory_space=pltpu.HBM),
        ],
        out_specs=(pl.BlockSpec(memory_space=pltpu.HBM), pl.BlockSpec(memory_space=pltpu.VMEM)),
        scratch_shapes=[
            pltpu.VMEM((inner, width), BF16),
            pltpu.VMEM((rows, width), BF16),
            pltpu.VMEM((rows, width), BF16),
            pltpu.VMEM((rows, EXTRA), F32),
            pltpu.VMEM((rows, inner), BF16),
            pltpu.VMEM(back_shape, BF16),
            pltpu.VMEM((experts * 8, 128), F32),
            pltpu.SemaphoreType.DMA((EXPERT_BLOCKS,)),
            pltpu.SemaphoreType.DMA((width // 2 // PIECE + 1,)),
        ],
        compiler_params=pltpu.CompilerParams(vmem_limit_bytes=EXPERT_VMEM),
    )(recv, w_in, w_out)


def weight_kernel(recv_ref, w_in_ref, w_out_ref, d_in_ref, d_out_ref, routed_ref, scaled_ref):
    width = routed_ref.shape[1]

    @pl.when(pl.program_id(0) == 0)
    def _():
        for k in range(0, width, PIECE):
            first, second = split_halves(recv_ref[:, k : k + PIECE])
            routed_ref[:, k : k + PIECE] = first
            scaled_ref[:, k : k + PIECE] = second

    pre = dot(routed_ref[...], w_in_ref[0])
    back = dot(scaled_ref[...], w_out_ref[0], 1, 1)
    hidden = jnp.maximum(pre, 0.0).astype(BF16)
    hgrad = jnp.where(pre > 0.0, back, 0.0).astype(BF16)
    d_in_ref[0] = dot(routed_ref[...], hgrad, 0, 0).astype(BF16)
    d_out_ref[0] = dot(hidden, scaled_ref[...], 0, 0).astype(BF16)


def weight_grads(recv, w_in, w_out):
    rows2, columns = recv.shape
    rows = rows2 // 2
    width, inner = w_in.shape[1:]
    block = inner // BLOCKS
    flops = 4 * 2 * rows * inner * width
    moved = 2 * (rows2 * columns + 4 * inner * width)
    in_block = pl.BlockSpec((1, width, block), lambda i: (0, 0, i))
    out_block = pl.BlockSpec((1, block, width), lambda i: (0, i, 0))
    return pl.pallas_call(
        weight_kernel,
        grid=(BLOCKS,),
        out_shape=(
            jax.ShapeDtypeStruct(w_in.shape, BF16),
            jax.ShapeDtypeStruct(w_out.shape, BF16),
        ),
        in_specs=[pl.BlockSpec((rows2, columns), lambda i: (0, 0)), in_block, out_block],
        out_specs=(in_block, out_block),
        scratch_shapes=[
            pltpu.VMEM((rows, width), BF16),
            pltpu.VMEM((rows, width), BF16),
        ],
        compiler_params=pltpu.CompilerParams(vmem_limit_bytes=WEIGHT_VMEM),
        cost_estimate=pl.CostEstimate(flops=flops, bytes_accessed=moved, transcendentals=0),
    )(recv, w_in, w_out)


def post_kernel(recv_ref, slot_ref, tok_ref, q_ref, own_ref, other_ref, odd_ref, d_tok_ref, d_router_ref):
    rows = recv_ref.shape[0]
    n_tok, width = d_tok_ref.shape
    half = width // 2
    row = iota((rows, n_tok), 0)
    slot = slot_ref[...]
    first = jnp.where(row == slot, 1.0, 0.0).astype(BF16)
    second = jnp.where(row == slot + CAP, 1.0, 0.0).astype(BF16)
    left = dot(first, recv_ref[:, 0:half], 0, 0)
    right = dot(second, recv_ref[:, 0:half], 0, 0)
    product = tok_ref[:, 0:half].astype(F32) * left + tok_ref[:, half:].astype(F32) * right
    c = jnp.sum(product, axis=1, keepdims=True)
    logit_grad = (c * q_ref[...].astype(F32)).astype(BF16)
    own = dot(logit_grad, own_ref[...])
    other = dot(logit_grad, other_ref[...])
    odd = odd_ref[...] > 0
    d_tok_ref[:, 0:half] = (left + jnp.where(odd, other, own)).astype(BF16)
    d_tok_ref[:, half:] = (right + jnp.where(odd, own, other)).astype(BF16)
    parts = recv_ref[:, half:].astype(F32).reshape(rows // 8, 8, 128)
    total = jnp.sum(parts, axis=0)
    for k in range(width // 128):
        d_router_ref[:, k * 128 : (k + 1) * 128] = total[k : k + 1, :]


def post(recv, slot, tokens, q, own, other, odd):
    n_tok, width = tokens.shape
    return pl.pallas_call(
        post_kernel,
        out_shape=(
            jax.ShapeDtypeStruct((n_tok, width), BF16),
            jax.ShapeDtypeStruct((1, width), F32),
        ),
        compiler_params=pltpu.CompilerParams(vmem_limit_bytes=POST_VMEM),
    )(recv, slot, tokens, q, own, other, odd)


def exchange(rows, experts):
    count, columns = rows.shape
    cut = rows.reshape(experts, count // experts, columns)
    return lax.all_to_all(cut, AXES, split_axis=0, concat_axis=0, tiled=True).reshape(count, columns)


def per_device(tokens, out_grad, expert_ids, router_logits, router_weight, w_in, w_out):
    experts = router_logits.shape[1]
    n_tok, width = tokens.shape
    send, slot, q = prep(
        expert_ids.reshape(1, n_tok), router_logits, tokens, out_grad, router_weight
    )
    recv = exchange(send, experts)
    back, own = expert(recv, w_in, w_out)
    got = exchange(back, experts)
    swap = [(i, i ^ 1) for i in range(lax.axis_size("col"))]
    other = lax.ppermute(own, "col", swap)
    odd = jnp.full((1, 1), lax.axis_index("col") % 2, jnp.int32)
    d_in, d_out = weight_grads(recv, w_in, w_out)
    d_tokens, d_router = post(got, slot, tokens, q, own, other, odd)
    return (d_tokens, d_in, d_out, d_router)


def solution(mesh):
    rows = P(AXES, None)
    cube = P(AXES, None, None)
    return jax.shard_map(
        per_device,
        mesh=mesh,
        in_specs=(rows, rows, P(AXES), rows, rows, cube, cube),
        out_specs=(rows, cube, cube, rows),
        check_vma=False,
    )
```

```python
import jax
import jax.numpy as jnp
from jax import lax
from jax.experimental import pallas as pl
from jax.experimental.pallas import tpu as pltpu
from jax.sharding import PartitionSpec as P

BF16 = jnp.bfloat16
F32 = jnp.float32
AXES = ("row", "col")
CAP = 4
EXTRA = 128
PIECE = 256
MIB = 1024 * 1024
PREP_VMEM = 63 * MIB
EXPERT_VMEM = 46 * MIB
WEIGHT_VMEM = 55 * MIB
POST_VMEM = 16 * MIB
EXPERT_BLOCKS = 2
BLOCKS = 4
PREP_PARTS = 8


def dot(a, b, ca=1, cb=0):
    return lax.dot_general(a, b, (((ca,), (cb,)), ((), ())), preferred_element_type=F32)


def iota(shape, axis):
    return lax.broadcasted_iota(jnp.int32, shape, axis)


def prep_kernel(
    ids_hbm, logits_hbm, tok_hbm, og_hbm, rw_hbm, send_hbm, slot_ref, q_ref,
    ids_ref, logits_ref, rhs_ref, og_ref, rw_ref, send_ref, sems, out_sems,
):
    n_tok, width = og_ref.shape
    experts = logits_ref.shape[1]
    rows = send_ref.shape[0]
    copies = [
        pltpu.make_async_copy(src, dst, sems.at[i])
        for i, (src, dst) in enumerate(
            [
                (ids_hbm, ids_ref),
                (logits_hbm, logits_ref),
                (og_hbm, og_ref),
                (tok_hbm, rhs_ref.at[pl.ds(0, n_tok), :]),
                (rw_hbm, rw_ref),
            ]
        )
    ]
    for copy in copies:
        copy.start()
    upper = jnp.where(iota((n_tok, n_tok), 0) < iota((n_tok, n_tok), 1), 1.0, 0.0).astype(BF16)
    copies[0].wait()
    ids = ids_ref[...]
    onehot_t = jnp.where(iota((experts, n_tok), 0) == ids, 1.0, 0.0).astype(F32)
    earlier = dot(onehot_t.astype(BF16), upper)
    rank = jnp.sum(earlier * onehot_t, axis=0, keepdims=True)
    slot = ids * (2 * CAP) + rank.astype(jnp.int32)
    slot_ref[...] = slot
    onehot = onehot_t.T
    copies[1].wait()
    logits = logits_ref[...]
    grown = jnp.exp(logits - jnp.max(logits, axis=1, keepdims=True))
    probs = grown / jnp.sum(grown, axis=1, keepdims=True)
    gate = jnp.sum(probs * onehot, axis=1, keepdims=True)
    q = (onehot - probs).astype(BF16)
    q_ref[...] = q
    copies[2].wait()
    rhs_ref[pl.ds(n_tok, n_tok), :] = (gate * og_ref[...].astype(F32)).astype(BF16)
    copies[3].wait()
    copies[4].wait()
    router = rw_ref[...].astype(F32)
    group = 4 * CAP
    place = iota((group, EXTRA), 0)
    pieces = jnp.zeros((group, EXTRA), F32)
    for k in range(2 * CAP):
        piece = jnp.broadcast_to(router[:, k * EXTRA : (k + 1) * EXTRA], (group, EXTRA))
        pieces = jnp.where(place == k + k // CAP * CAP, piece, pieces)
    part = rows // PREP_PARTS
    outs = []
    for start in range(0, rows, part):
        row = iota((part, n_tok), 0) + start
        first = jnp.where(row == slot, 1.0, 0.0).astype(BF16)
        second = jnp.where(row == slot + CAP, 1.0, 0.0).astype(BF16)
        both = jnp.concatenate([first, second], axis=1)
        send_ref[start : start + part, 0:width] = dot(both, rhs_ref[...]).astype(BF16)
        side = dot(second, q).reshape(part // group, group, EXTRA)
        side = side + pieces[None]
        send_ref[start : start + part, width:] = side.reshape(part, EXTRA).astype(BF16)
        out = pltpu.make_async_copy(
            send_ref.at[pl.ds(start, part), :],
            send_hbm.at[pl.ds(start, part), :],
            out_sems.at[start // part],
        )
        out.start()
        outs.append(out)
    for out in outs:
        out.wait()


def prep(ids, logits, tokens, out_grad, router_weight):
    n_tok, width = tokens.shape
    experts = logits.shape[1]
    rows = experts * 2 * CAP
    return pl.pallas_call(
        prep_kernel,
        out_shape=(
            jax.ShapeDtypeStruct((rows, width + EXTRA), BF16),
            jax.ShapeDtypeStruct((1, n_tok), jnp.int32),
            jax.ShapeDtypeStruct((n_tok, experts), BF16),
        ),
        in_specs=[pl.BlockSpec(memory_space=pltpu.HBM)] * 5,
        out_specs=(
            pl.BlockSpec(memory_space=pltpu.HBM),
            pl.BlockSpec(memory_space=pltpu.VMEM),
            pl.BlockSpec(memory_space=pltpu.VMEM),
        ),
        scratch_shapes=[
            pltpu.VMEM((1, n_tok), jnp.int32),
            pltpu.VMEM((n_tok, experts), F32),
            pltpu.VMEM((2 * n_tok, width), BF16),
            pltpu.VMEM((n_tok, width), BF16),
            pltpu.VMEM((1, width), BF16),
            pltpu.VMEM((rows, width + EXTRA), BF16),
            pltpu.SemaphoreType.DMA((5,)),
            pltpu.SemaphoreType.DMA((PREP_PARTS,)),
        ],
        compiler_params=pltpu.CompilerParams(vmem_limit_bytes=PREP_VMEM),
    )(ids, logits, tokens, out_grad, router_weight)


def split_halves(block):
    rows, columns = block.shape
    tiles = block.astype(F32).reshape(rows // 16, 2, 8, columns)
    even, odd = tiles[:, 0], tiles[:, 1]
    low = iota(even.shape, 1) < 4
    first = jnp.where(low, even, pltpu.roll(odd, 4, axis=1))
    second = jnp.where(low, pltpu.roll(even, 4, axis=1), odd)
    return first.reshape(rows // 2, columns).astype(BF16), second.reshape(rows // 2, columns).astype(BF16)


def join_halves(first, second):
    rows, columns = first.shape
    a = first.reshape(rows // 8, 8, columns)
    b = second.reshape(rows // 8, 8, columns)
    low = iota(a.shape, 1) < 4
    even = jnp.where(low, a, pltpu.roll(b, 4, axis=1))
    odd = jnp.where(low, pltpu.roll(a, 4, axis=1), b)
    return jnp.stack([even, odd], axis=1).reshape(2 * rows, columns)


def expert_kernel(
    recv_ref, w_in_ref, w_out_hbm, back_ref, router_ref,
    w_out_ref, routed_ref, scaled_ref, side_ref, hgrad_ref, part_ref, load_sems,
):
    rows, width = scaled_ref.shape
    inner = hgrad_ref.shape[1]
    experts = rows // CAP
    half = width // 2
    block = inner // EXPERT_BLOCKS
    loads = []
    for i in range(EXPERT_BLOCKS):
        cut = pl.ds(i * block, block)
        load = pltpu.make_async_copy(w_out_hbm.at[0, cut, :], w_out_ref.at[cut, :], load_sems.at[i])
        load.start()
        loads.append(load)
    for k in range(0, width, PIECE):
        first, second = split_halves(recv_ref[:, k : k + PIECE])
        routed_ref[:, k : k + PIECE] = first
        scaled_ref[:, k : k + PIECE] = second
    pieces, q = split_halves(recv_ref[:, width:])
    side_ref[...] = pieces.astype(F32)
    for k in range(CAP):
        strip = side_ref[pl.ds(k, experts, stride=CAP), :]
        router_ref[:, k * EXTRA : (k + 1) * EXTRA] = strip.astype(BF16)
    q = q.astype(F32)
    c = jnp.zeros((rows, 128), F32)
    pre_all = dot(routed_ref[...], w_in_ref[0])
    for i in range(EXPERT_BLOCKS):
        k = i * block
        pre = pre_all[:, k : k + block]
        loads[i].wait()
        back = dot(scaled_ref[...], w_out_ref[k : k + block, :], 1, 1)
        hgrad = jnp.where(pre > 0.0, back, 0.0)
        hgrad_ref[:, k : k + block] = hgrad.astype(BF16)
        product = pre * hgrad
        for j in range(0, block, 128):
            c = c + product[:, j : j + 128]
    logit_grad = (jnp.sum(c, axis=1, keepdims=True) * q).astype(BF16)

    def grad_piece(k):
        return dot(hgrad_ref[...], w_in_ref[0, k * PIECE : (k + 1) * PIECE, :], 1, 1)

    for k in range(half // PIECE):
        joined = join_halves(grad_piece(k), grad_piece(half // PIECE + k))
        back_ref[:, k * PIECE : (k + 1) * PIECE] = joined.astype(BF16)
    part = dot(logit_grad, routed_ref[...], 0, 0)
    for k in range(width // 128):
        part_ref[pl.ds(k, experts, stride=8), :] = part[:, k * 128 : (k + 1) * 128]
    back_ref[:, half:] = part_ref[...].astype(BF16)


def expert(recv, w_in, w_out):
    rows2, columns = recv.shape
    rows = rows2 // 2
    width, inner = w_in.shape[1:]
    experts = rows // CAP
    back_shape = (rows2, width // 2 + 128)
    return pl.pallas_call(
        expert_kernel,
        out_shape=(
            jax.ShapeDtypeStruct(back_shape, BF16),
            jax.ShapeDtypeStruct((experts, CAP * EXTRA), BF16),
        ),
        in_specs=[
            pl.BlockSpec(memory_space=pltpu.VMEM),
            pl.BlockSpec(memory_space=pltpu.VMEM),
            pl.BlockSpec(memory_space=pltpu.HBM),
        ],
        out_specs=(pl.BlockSpec(memory_space=pltpu.VMEM),) * 2,
        scratch_shapes=[
            pltpu.VMEM((inner, width), BF16),
            pltpu.VMEM((rows, width), BF16),
            pltpu.VMEM((rows, width), BF16),
            pltpu.VMEM((rows, EXTRA), F32),
            pltpu.VMEM((rows, inner), BF16),
            pltpu.VMEM((experts * 8, 128), F32),
            pltpu.SemaphoreType.DMA((EXPERT_BLOCKS,)),
        ],
        compiler_params=pltpu.CompilerParams(vmem_limit_bytes=EXPERT_VMEM),
    )(recv, w_in, w_out)


def weight_kernel(recv_ref, w_in_ref, w_out_ref, d_in_ref, d_out_ref, routed_ref, scaled_ref):
    width = routed_ref.shape[1]

    @pl.when(pl.program_id(0) == 0)
    def _():
        for k in range(0, width, PIECE):
            first, second = split_halves(recv_ref[:, k : k + PIECE])
            routed_ref[:, k : k + PIECE] = first
            scaled_ref[:, k : k + PIECE] = second

    pre = dot(routed_ref[...], w_in_ref[0])
    back = dot(scaled_ref[...], w_out_ref[0], 1, 1)
    hidden = jnp.maximum(pre, 0.0).astype(BF16)
    hgrad = jnp.where(pre > 0.0, back, 0.0).astype(BF16)
    d_in_ref[0] = dot(routed_ref[...], hgrad, 0, 0).astype(BF16)
    d_out_ref[0] = dot(hidden, scaled_ref[...], 0, 0).astype(BF16)


def weight_grads(recv, w_in, w_out):
    rows2, columns = recv.shape
    rows = rows2 // 2
    width, inner = w_in.shape[1:]
    block = inner // BLOCKS
    flops = 4 * 2 * rows * inner * width
    moved = 2 * (rows2 * columns + 4 * inner * width)
    in_block = pl.BlockSpec((1, width, block), lambda i: (0, 0, i))
    out_block = pl.BlockSpec((1, block, width), lambda i: (0, i, 0))
    return pl.pallas_call(
        weight_kernel,
        grid=(BLOCKS,),
        out_shape=(
            jax.ShapeDtypeStruct(w_in.shape, BF16),
            jax.ShapeDtypeStruct(w_out.shape, BF16),
        ),
        in_specs=[pl.BlockSpec((rows2, columns), lambda i: (0, 0)), in_block, out_block],
        out_specs=(in_block, out_block),
        scratch_shapes=[
            pltpu.VMEM((rows, width), BF16),
            pltpu.VMEM((rows, width), BF16),
        ],
        compiler_params=pltpu.CompilerParams(vmem_limit_bytes=WEIGHT_VMEM),
        cost_estimate=pl.CostEstimate(flops=flops, bytes_accessed=moved, transcendentals=0),
    )(recv, w_in, w_out)


def post_kernel(recv_ref, slot_ref, tok_ref, q_ref, own_ref, other_ref, odd_ref, d_tok_ref, d_router_ref):
    rows = recv_ref.shape[0]
    n_tok, width = d_tok_ref.shape
    half = width // 2
    row = iota((rows, n_tok), 0)
    slot = slot_ref[...]
    first = jnp.where(row == slot, 1.0, 0.0).astype(BF16)
    second = jnp.where(row == slot + CAP, 1.0, 0.0).astype(BF16)
    left = dot(first, recv_ref[:, 0:half], 0, 0)
    right = dot(second, recv_ref[:, 0:half], 0, 0)
    product = tok_ref[:, 0:half].astype(F32) * left + tok_ref[:, half:].astype(F32) * right
    c = jnp.sum(product, axis=1, keepdims=True)
    logit_grad = (c * q_ref[...].astype(F32)).astype(BF16)
    own = dot(logit_grad, own_ref[...])
    other = dot(logit_grad, other_ref[...])
    odd = odd_ref[...] > 0
    d_tok_ref[:, 0:half] = (left + jnp.where(odd, other, own)).astype(BF16)
    d_tok_ref[:, half:] = (right + jnp.where(odd, own, other)).astype(BF16)
    parts = recv_ref[:, half:].astype(F32).reshape(rows // 8, 8, 128)
    total = jnp.sum(parts, axis=0)
    for k in range(width // 128):
        d_router_ref[:, k * 128 : (k + 1) * 128] = total[k : k + 1, :]


def post(recv, slot, tokens, q, own, other, odd):
    n_tok, width = tokens.shape
    return pl.pallas_call(
        post_kernel,
        out_shape=(
            jax.ShapeDtypeStruct((n_tok, width), BF16),
            jax.ShapeDtypeStruct((1, width), F32),
        ),
        compiler_params=pltpu.CompilerParams(vmem_limit_bytes=POST_VMEM),
    )(recv, slot, tokens, q, own, other, odd)


def exchange(rows, experts):
    count, columns = rows.shape
    cut = rows.reshape(experts, count // experts, columns)
    return lax.all_to_all(cut, AXES, split_axis=0, concat_axis=0, tiled=True).reshape(count, columns)


def per_device(tokens, out_grad, expert_ids, router_logits, router_weight, w_in, w_out):
    experts = router_logits.shape[1]
    n_tok, width = tokens.shape
    send, slot, q = prep(
        expert_ids.reshape(1, n_tok), router_logits, tokens, out_grad, router_weight
    )
    recv = exchange(send, experts)
    back, own = expert(recv, w_in, w_out)
    got = exchange(back, experts)
    swap = [(i, i ^ 1) for i in range(lax.axis_size("col"))]
    other = lax.ppermute(own, "col", swap)
    odd = jnp.full((1, 1), lax.axis_index("col") % 2, jnp.int32)
    d_in, d_out = weight_grads(recv, w_in, w_out)
    d_tokens, d_router = post(got, slot, tokens, q, own, other, odd)
    return (d_tokens, d_in, d_out, d_router)


def solution(mesh):
    rows = P(AXES, None)
    cube = P(AXES, None, None)
    return jax.shard_map(
        per_device,
        mesh=mesh,
        in_specs=(rows, rows, P(AXES), rows, rows, cube, cube),
        out_specs=(rows, cube, cube, rows),
        check_vma=False,
    )
```

```python
import jax
import jax.numpy as jnp
from jax import lax
from jax.experimental import pallas as pl
from jax.experimental.pallas import tpu as pltpu
from jax.sharding import PartitionSpec as P

BF16 = jnp.bfloat16
F32 = jnp.float32
AXES = ("row", "col")
CAP = 4
EXTRA = 128
PIECE = 256
MIB = 1024 * 1024
PREP_VMEM = 63 * MIB
EXPERT_VMEM = 46 * MIB
WEIGHT_VMEM = 55 * MIB
POST_VMEM = 16 * MIB
EXPERT_BLOCKS = 2
BLOCKS = 4
PREP_PARTS = 8


def dot(a, b, ca=1, cb=0):
    return lax.dot_general(a, b, (((ca,), (cb,)), ((), ())), preferred_element_type=F32)


def iota(shape, axis):
    return lax.broadcasted_iota(jnp.int32, shape, axis)


def prep_kernel(
    ids_hbm, logits_hbm, tok_hbm, og_hbm, rw_hbm, send_hbm, slot_hbm, q_hbm,
    ids_ref, logits_ref, rhs_ref, og_ref, rw_ref, send_ref, slot_ref, q_ref, sems, out_sems,
):
    n_tok, width = og_ref.shape
    experts = logits_ref.shape[1]
    rows = send_ref.shape[0]
    copies = [
        pltpu.make_async_copy(src, dst, sems.at[i])
        for i, (src, dst) in enumerate(
            [
                (ids_hbm, ids_ref),
                (logits_hbm, logits_ref),
                (og_hbm, og_ref),
                (tok_hbm, rhs_ref.at[pl.ds(0, n_tok), :]),
                (rw_hbm, rw_ref),
            ]
        )
    ]
    for copy in copies:
        copy.start()
    upper = jnp.where(iota((n_tok, n_tok), 0) < iota((n_tok, n_tok), 1), 1.0, 0.0).astype(BF16)
    copies[0].wait()
    ids = ids_ref[...]
    onehot_t = jnp.where(iota((experts, n_tok), 0) == ids, 1.0, 0.0).astype(F32)
    earlier = dot(onehot_t.astype(BF16), upper)
    rank = jnp.sum(earlier * onehot_t, axis=0, keepdims=True)
    slot = ids * (2 * CAP) + rank.astype(jnp.int32)
    slot_ref[...] = slot
    outs = [pltpu.make_async_copy(slot_ref, slot_hbm, out_sems.at[PREP_PARTS])]
    outs[0].start()
    onehot = onehot_t.T
    copies[1].wait()
    logits = logits_ref[...]
    grown = jnp.exp(logits - jnp.max(logits, axis=1, keepdims=True))
    probs = grown / jnp.sum(grown, axis=1, keepdims=True)
    gate = jnp.sum(probs * onehot, axis=1, keepdims=True)
    q = (onehot - probs).astype(BF16)
    q_ref[...] = q
    outs.append(pltpu.make_async_copy(q_ref, q_hbm, out_sems.at[PREP_PARTS + 1]))
    outs[1].start()
    copies[2].wait()
    rhs_ref[pl.ds(n_tok, n_tok), :] = (gate * og_ref[...].astype(F32)).astype(BF16)
    copies[3].wait()
    copies[4].wait()
    router = rw_ref[...].astype(F32)
    group = 4 * CAP
    place = iota((group, EXTRA), 0)
    pieces = jnp.zeros((group, EXTRA), F32)
    for k in range(2 * CAP):
        piece = jnp.broadcast_to(router[:, k * EXTRA : (k + 1) * EXTRA], (group, EXTRA))
        pieces = jnp.where(place == k + k // CAP * CAP, piece, pieces)
    part = rows // PREP_PARTS
    for start in range(0, rows, part):
        row = iota((part, n_tok), 0) + start
        first = jnp.where(row == slot, 1.0, 0.0).astype(BF16)
        second = jnp.where(row == slot + CAP, 1.0, 0.0).astype(BF16)
        both = jnp.concatenate([first, second], axis=1)
        send_ref[start : start + part, 0:width] = dot(both, rhs_ref[...]).astype(BF16)
        side = dot(second, q).reshape(part // group, group, EXTRA)
        side = side + pieces[None]
        send_ref[start : start + part, width:] = side.reshape(part, EXTRA).astype(BF16)
        out = pltpu.make_async_copy(
            send_ref.at[pl.ds(start, part), :],
            send_hbm.at[pl.ds(start, part), :],
            out_sems.at[start // part],
        )
        out.start()
        outs.append(out)
    for out in outs:
        out.wait()


def prep(ids, logits, tokens, out_grad, router_weight):
    n_tok, width = tokens.shape
    experts = logits.shape[1]
    rows = experts * 2 * CAP
    return pl.pallas_call(
        prep_kernel,
        out_shape=(
            jax.ShapeDtypeStruct((rows, width + EXTRA), BF16),
            jax.ShapeDtypeStruct((1, n_tok), jnp.int32),
            jax.ShapeDtypeStruct((n_tok, experts), BF16),
        ),
        in_specs=[pl.BlockSpec(memory_space=pltpu.HBM)] * 5,
        out_specs=(
            pl.BlockSpec(memory_space=pltpu.HBM),
            pl.BlockSpec(memory_space=pltpu.HBM),
            pl.BlockSpec(memory_space=pltpu.HBM),
        ),
        scratch_shapes=[
            pltpu.VMEM((1, n_tok), jnp.int32),
            pltpu.VMEM((n_tok, experts), F32),
            pltpu.VMEM((2 * n_tok, width), BF16),
            pltpu.VMEM((n_tok, width), BF16),
            pltpu.VMEM((1, width), BF16),
            pltpu.VMEM((rows, width + EXTRA), BF16),
            pltpu.VMEM((1, n_tok), jnp.int32),
            pltpu.VMEM((n_tok, experts), BF16),
            pltpu.SemaphoreType.DMA((5,)),
            pltpu.SemaphoreType.DMA((PREP_PARTS + 2,)),
        ],
        compiler_params=pltpu.CompilerParams(vmem_limit_bytes=PREP_VMEM),
    )(ids, logits, tokens, out_grad, router_weight)


def split_halves(block):
    rows, columns = block.shape
    tiles = block.astype(F32).reshape(rows // 16, 2, 8, columns)
    even, odd = tiles[:, 0], tiles[:, 1]
    low = iota(even.shape, 1) < 4
    first = jnp.where(low, even, pltpu.roll(odd, 4, axis=1))
    second = jnp.where(low, pltpu.roll(even, 4, axis=1), odd)
    return first.reshape(rows // 2, columns).astype(BF16), second.reshape(rows // 2, columns).astype(BF16)


def join_halves(first, second):
    rows, columns = first.shape
    a = first.reshape(rows // 8, 8, columns)
    b = second.reshape(rows // 8, 8, columns)
    low = iota(a.shape, 1) < 4
    even = jnp.where(low, a, pltpu.roll(b, 4, axis=1))
    odd = jnp.where(low, pltpu.roll(a, 4, axis=1), b)
    return jnp.stack([even, odd], axis=1).reshape(2 * rows, columns)


def expert_kernel(
    recv_ref, w_in_ref, w_out_hbm, back_ref, router_ref,
    w_out_ref, routed_ref, scaled_ref, side_ref, hgrad_ref, part_ref, load_sems,
):
    rows, width = scaled_ref.shape
    inner = hgrad_ref.shape[1]
    experts = rows // CAP
    half = width // 2
    block = inner // EXPERT_BLOCKS
    loads = []
    for i in range(EXPERT_BLOCKS):
        cut = pl.ds(i * block, block)
        load = pltpu.make_async_copy(w_out_hbm.at[0, cut, :], w_out_ref.at[cut, :], load_sems.at[i])
        load.start()
        loads.append(load)
    for k in range(0, width, PIECE):
        first, second = split_halves(recv_ref[:, k : k + PIECE])
        routed_ref[:, k : k + PIECE] = first
        scaled_ref[:, k : k + PIECE] = second
    pieces, q = split_halves(recv_ref[:, width:])
    side_ref[...] = pieces.astype(F32)
    for k in range(CAP):
        strip = side_ref[pl.ds(k, experts, stride=CAP), :]
        router_ref[:, k * EXTRA : (k + 1) * EXTRA] = strip.astype(BF16)
    q = q.astype(F32)
    c = jnp.zeros((rows, 128), F32)
    pre_all = dot(routed_ref[...], w_in_ref[0])
    for i in range(EXPERT_BLOCKS):
        k = i * block
        pre = pre_all[:, k : k + block]
        loads[i].wait()
        back = dot(scaled_ref[...], w_out_ref[k : k + block, :], 1, 1)
        hgrad = jnp.where(pre > 0.0, back, 0.0)
        hgrad_ref[:, k : k + block] = hgrad.astype(BF16)
        product = pre * hgrad
        for j in range(0, block, 128):
            c = c + product[:, j : j + 128]
    logit_grad = (jnp.sum(c, axis=1, keepdims=True) * q).astype(BF16)

    def grad_piece(k):
        return dot(hgrad_ref[...], w_in_ref[0, k * PIECE : (k + 1) * PIECE, :], 1, 1)

    for k in range(half // PIECE):
        joined = join_halves(grad_piece(k), grad_piece(half // PIECE + k))
        back_ref[:, k * PIECE : (k + 1) * PIECE] = joined.astype(BF16)
    part = dot(logit_grad, routed_ref[...], 0, 0)
    for k in range(width // 128):
        part_ref[pl.ds(k, experts, stride=8), :] = part[:, k * 128 : (k + 1) * 128]
    back_ref[:, half:] = part_ref[...].astype(BF16)


def expert(recv, w_in, w_out):
    rows2, columns = recv.shape
    rows = rows2 // 2
    width, inner = w_in.shape[1:]
    experts = rows // CAP
    back_shape = (rows2, width // 2 + 128)
    return pl.pallas_call(
        expert_kernel,
        out_shape=(
            jax.ShapeDtypeStruct(back_shape, BF16),
            jax.ShapeDtypeStruct((experts, CAP * EXTRA), BF16),
        ),
        in_specs=[
            pl.BlockSpec(memory_space=pltpu.VMEM),
            pl.BlockSpec(memory_space=pltpu.VMEM),
            pl.BlockSpec(memory_space=pltpu.HBM),
        ],
        out_specs=(pl.BlockSpec(memory_space=pltpu.VMEM),) * 2,
        scratch_shapes=[
            pltpu.VMEM((inner, width), BF16),
            pltpu.VMEM((rows, width), BF16),
            pltpu.VMEM((rows, width), BF16),
            pltpu.VMEM((rows, EXTRA), F32),
            pltpu.VMEM((rows, inner), BF16),
            pltpu.VMEM((experts * 8, 128), F32),
            pltpu.SemaphoreType.DMA((EXPERT_BLOCKS,)),
        ],
        compiler_params=pltpu.CompilerParams(vmem_limit_bytes=EXPERT_VMEM),
    )(recv, w_in, w_out)


def weight_kernel(recv_ref, w_in_ref, w_out_ref, d_in_ref, d_out_ref, routed_ref, scaled_ref):
    width = routed_ref.shape[1]

    @pl.when(pl.program_id(0) == 0)
    def _():
        for k in range(0, width, PIECE):
            first, second = split_halves(recv_ref[:, k : k + PIECE])
            routed_ref[:, k : k + PIECE] = first
            scaled_ref[:, k : k + PIECE] = second

    pre = dot(routed_ref[...], w_in_ref[0])
    back = dot(scaled_ref[...], w_out_ref[0], 1, 1)
    hidden = jnp.maximum(pre, 0.0).astype(BF16)
    hgrad = jnp.where(pre > 0.0, back, 0.0).astype(BF16)
    d_in_ref[0] = dot(routed_ref[...], hgrad, 0, 0).astype(BF16)
    d_out_ref[0] = dot(hidden, scaled_ref[...], 0, 0).astype(BF16)


def weight_grads(recv, w_in, w_out):
    rows2, columns = recv.shape
    rows = rows2 // 2
    width, inner = w_in.shape[1:]
    block = inner // BLOCKS
    flops = 4 * 2 * rows * inner * width
    moved = 2 * (rows2 * columns + 4 * inner * width)
    in_block = pl.BlockSpec((1, width, block), lambda i: (0, 0, i))
    out_block = pl.BlockSpec((1, block, width), lambda i: (0, i, 0))
    return pl.pallas_call(
        weight_kernel,
        grid=(BLOCKS,),
        out_shape=(
            jax.ShapeDtypeStruct(w_in.shape, BF16),
            jax.ShapeDtypeStruct(w_out.shape, BF16),
        ),
        in_specs=[pl.BlockSpec((rows2, columns), lambda i: (0, 0)), in_block, out_block],
        out_specs=(in_block, out_block),
        scratch_shapes=[
            pltpu.VMEM((rows, width), BF16),
            pltpu.VMEM((rows, width), BF16),
        ],
        compiler_params=pltpu.CompilerParams(vmem_limit_bytes=WEIGHT_VMEM),
        cost_estimate=pl.CostEstimate(flops=flops, bytes_accessed=moved, transcendentals=0),
    )(recv, w_in, w_out)


def post_kernel(recv_ref, slot_ref, tok_ref, q_ref, own_ref, other_ref, odd_ref, d_tok_ref, d_router_ref):
    rows = recv_ref.shape[0]
    n_tok, width = d_tok_ref.shape
    half = width // 2
    row = iota((rows, n_tok), 0)
    slot = slot_ref[...]
    first = jnp.where(row == slot, 1.0, 0.0).astype(BF16)
    second = jnp.where(row == slot + CAP, 1.0, 0.0).astype(BF16)
    left = dot(first, recv_ref[:, 0:half], 0, 0)
    right = dot(second, recv_ref[:, 0:half], 0, 0)
    product = tok_ref[:, 0:half].astype(F32) * left + tok_ref[:, half:].astype(F32) * right
    c = jnp.sum(product, axis=1, keepdims=True)
    logit_grad = (c * q_ref[...].astype(F32)).astype(BF16)
    own = dot(logit_grad, own_ref[...])
    other = dot(logit_grad, other_ref[...])
    odd = odd_ref[...] > 0
    d_tok_ref[:, 0:half] = (left + jnp.where(odd, other, own)).astype(BF16)
    d_tok_ref[:, half:] = (right + jnp.where(odd, own, other)).astype(BF16)
    parts = recv_ref[:, half:].astype(F32).reshape(rows // 8, 8, 128)
    total = jnp.sum(parts, axis=0)
    for k in range(width // 128):
        d_router_ref[:, k * 128 : (k + 1) * 128] = total[k : k + 1, :]


def post(recv, slot, tokens, q, own, other, odd):
    n_tok, width = tokens.shape
    return pl.pallas_call(
        post_kernel,
        out_shape=(
            jax.ShapeDtypeStruct((n_tok, width), BF16),
            jax.ShapeDtypeStruct((1, width), F32),
        ),
        compiler_params=pltpu.CompilerParams(vmem_limit_bytes=POST_VMEM),
    )(recv, slot, tokens, q, own, other, odd)


def exchange(rows, experts):
    count, columns = rows.shape
    cut = rows.reshape(experts, count // experts, columns)
    return lax.all_to_all(cut, AXES, split_axis=0, concat_axis=0, tiled=True).reshape(count, columns)


def per_device(tokens, out_grad, expert_ids, router_logits, router_weight, w_in, w_out):
    experts = router_logits.shape[1]
    n_tok, width = tokens.shape
    send, slot, q = prep(
        expert_ids.reshape(1, n_tok), router_logits, tokens, out_grad, router_weight
    )
    recv = exchange(send, experts)
    back, own = expert(recv, w_in, w_out)
    got = exchange(back, experts)
    swap = [(i, i ^ 1) for i in range(lax.axis_size("col"))]
    other = lax.ppermute(own, "col", swap)
    odd = jnp.full((1, 1), lax.axis_index("col") % 2, jnp.int32)
    d_in, d_out = weight_grads(recv, w_in, w_out)
    d_tokens, d_router = post(got, slot, tokens, q, own, other, odd)
    return (d_tokens, d_in, d_out, d_router)


def solution(mesh):
    rows = P(AXES, None)
    cube = P(AXES, None, None)
    return jax.shard_map(
        per_device,
        mesh=mesh,
        in_specs=(rows, rows, P(AXES), rows, rows, cube, cube),
        out_specs=(rows, cube, cube, rows),
        check_vma=False,
    )
```

```python
import jax
import jax.numpy as jnp
from jax import lax
from jax.experimental import pallas as pl
from jax.experimental.pallas import tpu as pltpu
from jax.sharding import PartitionSpec as P

BF16 = jnp.bfloat16
F32 = jnp.float32
AXES = ("row", "col")
CAP = 4
EXTRA = 128
PIECE = 256
MIB = 1024 * 1024
PREP_VMEM = 63 * MIB
EXPERT_VMEM = 46 * MIB
WEIGHT_VMEM = 55 * MIB
POST_VMEM = 16 * MIB
EXPERT_BLOCKS = 2
BLOCKS = 4
PREP_PARTS = 8


def dot(a, b, ca=1, cb=0):
    return lax.dot_general(a, b, (((ca,), (cb,)), ((), ())), preferred_element_type=F32)


def iota(shape, axis):
    return lax.broadcasted_iota(jnp.int32, shape, axis)


def prep_kernel(
    ids_hbm, logits_hbm, tok_hbm, og_hbm, rw_hbm, send_hbm, slot_hbm, q_hbm,
    ids_ref, logits_ref, rhs_ref, og_ref, rw_ref, send_ref, slot_ref, q_ref, sems, out_sems,
):
    n_tok, width = og_ref.shape
    experts = logits_ref.shape[1]
    rows = send_ref.shape[0]
    copies = [
        pltpu.make_async_copy(src, dst, sems.at[i])
        for i, (src, dst) in enumerate(
            [
                (ids_hbm, ids_ref),
                (logits_hbm, logits_ref),
                (og_hbm, og_ref),
                (tok_hbm, rhs_ref.at[pl.ds(0, n_tok), :]),
                (rw_hbm, rw_ref),
            ]
        )
    ]
    for copy in copies:
        copy.start()
    upper = jnp.where(iota((n_tok, n_tok), 0) < iota((n_tok, n_tok), 1), 1.0, 0.0).astype(BF16)
    copies[0].wait()
    ids = ids_ref[...]
    onehot_t = jnp.where(iota((experts, n_tok), 0) == ids, 1.0, 0.0).astype(F32)
    earlier = dot(onehot_t.astype(BF16), upper)
    rank = jnp.sum(earlier * onehot_t, axis=0, keepdims=True)
    slot = ids * (2 * CAP) + rank.astype(jnp.int32)
    slot_ref[...] = slot
    outs = [pltpu.make_async_copy(slot_ref, slot_hbm, out_sems.at[PREP_PARTS])]
    outs[0].start()
    onehot = onehot_t.T
    copies[1].wait()
    logits = logits_ref[...]
    grown = jnp.exp(logits - jnp.max(logits, axis=1, keepdims=True))
    probs = grown / jnp.sum(grown, axis=1, keepdims=True)
    gate = jnp.sum(probs * onehot, axis=1, keepdims=True)
    q = (onehot - probs).astype(BF16)
    q_ref[...] = q
    outs.append(pltpu.make_async_copy(q_ref, q_hbm, out_sems.at[PREP_PARTS + 1]))
    outs[1].start()
    copies[2].wait()
    rhs_ref[pl.ds(n_tok, n_tok), :] = (gate * og_ref[...].astype(F32)).astype(BF16)
    copies[3].wait()
    copies[4].wait()
    router = rw_ref[...].astype(F32)
    group = 4 * CAP
    place = iota((group, EXTRA), 0)
    pieces = jnp.zeros((group, EXTRA), F32)
    for k in range(2 * CAP):
        piece = jnp.broadcast_to(router[:, k * EXTRA : (k + 1) * EXTRA], (group, EXTRA))
        pieces = jnp.where(place == k + k // CAP * CAP, piece, pieces)
    part = rows // PREP_PARTS
    for start in range(0, rows, part):
        row = iota((part, n_tok), 0) + start
        first = jnp.where(row == slot, 1.0, 0.0).astype(BF16)
        second = jnp.where(row == slot + CAP, 1.0, 0.0).astype(BF16)
        both = jnp.concatenate([first, second], axis=1)
        send_ref[start : start + part, 0:width] = dot(both, rhs_ref[...]).astype(BF16)
        side = dot(second, q).reshape(part // group, group, EXTRA)
        side = side + pieces[None]
        send_ref[start : start + part, width:] = side.reshape(part, EXTRA).astype(BF16)
        out = pltpu.make_async_copy(
            send_ref.at[pl.ds(start, part), :],
            send_hbm.at[pl.ds(start, part), :],
            out_sems.at[start // part],
        )
        out.start()
        outs.append(out)
    for out in outs:
        out.wait()


def prep(ids, logits, tokens, out_grad, router_weight):
    n_tok, width = tokens.shape
    experts = logits.shape[1]
    rows = experts * 2 * CAP
    return pl.pallas_call(
        prep_kernel,
        out_shape=(
            jax.ShapeDtypeStruct((rows, width + EXTRA), BF16),
            jax.ShapeDtypeStruct((1, n_tok), jnp.int32),
            jax.ShapeDtypeStruct((n_tok, experts), BF16),
        ),
        in_specs=[pl.BlockSpec(memory_space=pltpu.HBM)] * 5,
        out_specs=(
            pl.BlockSpec(memory_space=pltpu.HBM),
            pl.BlockSpec(memory_space=pltpu.HBM),
            pl.BlockSpec(memory_space=pltpu.HBM),
        ),
        scratch_shapes=[
            pltpu.VMEM((1, n_tok), jnp.int32),
            pltpu.VMEM((n_tok, experts), F32),
            pltpu.VMEM((2 * n_tok, width), BF16),
            pltpu.VMEM((n_tok, width), BF16),
            pltpu.VMEM((1, width), BF16),
            pltpu.VMEM((rows, width + EXTRA), BF16),
            pltpu.VMEM((1, n_tok), jnp.int32),
            pltpu.VMEM((n_tok, experts), BF16),
            pltpu.SemaphoreType.DMA((5,)),
            pltpu.SemaphoreType.DMA((PREP_PARTS + 2,)),
        ],
        compiler_params=pltpu.CompilerParams(vmem_limit_bytes=PREP_VMEM),
    )(ids, logits, tokens, out_grad, router_weight)


def split_halves(block):
    rows, columns = block.shape
    tiles = block.astype(F32).reshape(rows // 16, 2, 8, columns)
    even, odd = tiles[:, 0], tiles[:, 1]
    low = iota(even.shape, 1) < 4
    first = jnp.where(low, even, pltpu.roll(odd, 4, axis=1))
    second = jnp.where(low, pltpu.roll(even, 4, axis=1), odd)
    return first.reshape(rows // 2, columns).astype(BF16), second.reshape(rows // 2, columns).astype(BF16)


def join_halves(first, second):
    rows, columns = first.shape
    a = first.reshape(rows // 8, 8, columns)
    b = second.reshape(rows // 8, 8, columns)
    low = iota(a.shape, 1) < 4
    even = jnp.where(low, a, pltpu.roll(b, 4, axis=1))
    odd = jnp.where(low, pltpu.roll(a, 4, axis=1), b)
    return jnp.stack([even, odd], axis=1).reshape(2 * rows, columns)


def expert_kernel(
    recv_ref, w_in_ref, w_out_hbm, back_ref, router_ref,
    w_out_ref, routed_ref, scaled_ref, side_ref, hgrad_ref, part_ref, load_sems,
):
    rows, width = scaled_ref.shape
    inner = hgrad_ref.shape[1]
    experts = rows // CAP
    half = width // 2
    block = inner // EXPERT_BLOCKS
    loads = []
    for i in range(EXPERT_BLOCKS):
        cut = pl.ds(i * block, block)
        load = pltpu.make_async_copy(w_out_hbm.at[0, cut, :], w_out_ref.at[cut, :], load_sems.at[i])
        load.start()
        loads.append(load)
    for k in range(0, width, PIECE):
        first, second = split_halves(recv_ref[:, k : k + PIECE])
        routed_ref[:, k : k + PIECE] = first
        scaled_ref[:, k : k + PIECE] = second
    pieces, q = split_halves(recv_ref[:, width:])
    side_ref[...] = pieces.astype(F32)
    for k in range(CAP):
        strip = side_ref[pl.ds(k, experts, stride=CAP), :]
        router_ref[:, k * EXTRA : (k + 1) * EXTRA] = strip.astype(BF16)
    q = q.astype(F32)
    c = jnp.zeros((rows, 128), F32)
    pre_all = dot(routed_ref[...], w_in_ref[0])
    for i in range(EXPERT_BLOCKS):
        k = i * block
        pre = pre_all[:, k : k + block]
        loads[i].wait()
        back = dot(scaled_ref[...], w_out_ref[k : k + block, :], 1, 1)
        hgrad = jnp.where(pre > 0.0, back, 0.0)
        hgrad_ref[:, k : k + block] = hgrad.astype(BF16)
        product = pre * hgrad
        for j in range(0, block, 128):
            c = c + product[:, j : j + 128]
    logit_grad = (jnp.sum(c, axis=1, keepdims=True) * q).astype(BF16)

    def grad_piece(k):
        return dot(hgrad_ref[...], w_in_ref[0, k * PIECE : (k + 1) * PIECE, :], 1, 1)

    for k in range(half // PIECE):
        joined = join_halves(grad_piece(k), grad_piece(half // PIECE + k))
        back_ref[:, k * PIECE : (k + 1) * PIECE] = joined.astype(BF16)
    part = dot(logit_grad, routed_ref[...], 0, 0)
    for k in range(width // 128):
        part_ref[pl.ds(k, experts, stride=8), :] = part[:, k * 128 : (k + 1) * 128]
    back_ref[:, half:] = part_ref[...].astype(BF16)


def expert(recv, w_in, w_out):
    rows2, columns = recv.shape
    rows = rows2 // 2
    width, inner = w_in.shape[1:]
    experts = rows // CAP
    back_shape = (rows2, width // 2 + 128)
    return pl.pallas_call(
        expert_kernel,
        out_shape=(
            jax.ShapeDtypeStruct(back_shape, BF16),
            jax.ShapeDtypeStruct((experts, CAP * EXTRA), BF16),
        ),
        in_specs=[
            pl.BlockSpec(memory_space=pltpu.VMEM),
            pl.BlockSpec(memory_space=pltpu.VMEM),
            pl.BlockSpec(memory_space=pltpu.HBM),
        ],
        out_specs=(pl.BlockSpec(memory_space=pltpu.VMEM),) * 2,
        scratch_shapes=[
            pltpu.VMEM((inner, width), BF16),
            pltpu.VMEM((rows, width), BF16),
            pltpu.VMEM((rows, width), BF16),
            pltpu.VMEM((rows, EXTRA), F32),
            pltpu.VMEM((rows, inner), BF16),
            pltpu.VMEM((experts * 8, 128), F32),
            pltpu.SemaphoreType.DMA((EXPERT_BLOCKS,)),
        ],
        compiler_params=pltpu.CompilerParams(vmem_limit_bytes=EXPERT_VMEM),
    )(recv, w_in, w_out)


def weight_kernel(recv_ref, w_in_ref, w_out_ref, d_in_ref, d_out_ref, routed_ref, scaled_ref):
    width = routed_ref.shape[1]

    @pl.when(pl.program_id(0) == 0)
    def _():
        for k in range(0, width, PIECE):
            first, second = split_halves(recv_ref[:, k : k + PIECE])
            routed_ref[:, k : k + PIECE] = first
            scaled_ref[:, k : k + PIECE] = second

    pre = dot(routed_ref[...], w_in_ref[0])
    back = dot(scaled_ref[...], w_out_ref[0], 1, 1)
    hidden = jnp.maximum(pre, 0.0).astype(BF16)
    hgrad = jnp.where(pre > 0.0, back, 0.0).astype(BF16)
    d_in_ref[0] = dot(routed_ref[...], hgrad, 0, 0).astype(BF16)
    d_out_ref[0] = dot(hidden, scaled_ref[...], 0, 0).astype(BF16)


def weight_grads(recv, w_in, w_out):
    rows2, columns = recv.shape
    rows = rows2 // 2
    width, inner = w_in.shape[1:]
    block = inner // BLOCKS
    flops = 4 * 2 * rows * inner * width
    moved = 2 * (rows2 * columns + 4 * inner * width)
    in_block = pl.BlockSpec((1, width, block), lambda i: (0, 0, i))
    out_block = pl.BlockSpec((1, block, width), lambda i: (0, i, 0))
    return pl.pallas_call(
        weight_kernel,
        grid=(BLOCKS,),
        out_shape=(
            jax.ShapeDtypeStruct(w_in.shape, BF16),
            jax.ShapeDtypeStruct(w_out.shape, BF16),
        ),
        in_specs=[pl.BlockSpec((rows2, columns), lambda i: (0, 0)), in_block, out_block],
        out_specs=(in_block, out_block),
        scratch_shapes=[
            pltpu.VMEM((rows, width), BF16),
            pltpu.VMEM((rows, width), BF16),
        ],
        compiler_params=pltpu.CompilerParams(vmem_limit_bytes=WEIGHT_VMEM),
        cost_estimate=pl.CostEstimate(flops=flops, bytes_accessed=moved, transcendentals=0),
    )(recv, w_in, w_out)


def post_kernel(recv_ref, slot_ref, tok_ref, q_ref, own_ref, other_ref, odd_ref, d_tok_hbm, d_router_ref, d_tok_ref, sems):
    rows = recv_ref.shape[0]
    n_tok, width = d_tok_ref.shape
    half = width // 2
    row = iota((rows, n_tok), 0)
    slot = slot_ref[...]
    first = jnp.where(row == slot, 1.0, 0.0).astype(BF16)
    second = jnp.where(row == slot + CAP, 1.0, 0.0).astype(BF16)
    left = dot(first, recv_ref[:, 0:half], 0, 0)
    right = dot(second, recv_ref[:, 0:half], 0, 0)
    product = tok_ref[:, 0:half].astype(F32) * left + tok_ref[:, half:].astype(F32) * right
    c = jnp.sum(product, axis=1, keepdims=True)
    logit_grad = (c * q_ref[...].astype(F32)).astype(BF16)
    own = dot(logit_grad, own_ref[...])
    other = dot(logit_grad, other_ref[...])
    odd = odd_ref[...] > 0
    d_tok_ref[:, 0:half] = (left + jnp.where(odd, other, own)).astype(BF16)
    outs = [
        pltpu.make_async_copy(d_tok_ref.at[:, cut], d_tok_hbm.at[:, cut], sems.at[i])
        for i, cut in enumerate((pl.ds(0, half), pl.ds(half, half)))
    ]
    outs[0].start()
    d_tok_ref[:, half:] = (right + jnp.where(odd, own, other)).astype(BF16)
    outs[1].start()
    parts = recv_ref[:, half:].astype(F32).reshape(rows // 8, 8, 128)
    total = jnp.sum(parts, axis=0)
    for k in range(width // 128):
        d_router_ref[:, k * 128 : (k + 1) * 128] = total[k : k + 1, :]
    for out in outs:
        out.wait()


def post(recv, slot, tokens, q, own, other, odd):
    n_tok, width = tokens.shape
    return pl.pallas_call(
        post_kernel,
        out_shape=(
            jax.ShapeDtypeStruct((n_tok, width), BF16),
            jax.ShapeDtypeStruct((1, width), F32),
        ),
        in_specs=[pl.BlockSpec(memory_space=pltpu.VMEM)] * 7,
        out_specs=(pl.BlockSpec(memory_space=pltpu.HBM), pl.BlockSpec(memory_space=pltpu.VMEM)),
        scratch_shapes=[pltpu.VMEM((n_tok, width), BF16), pltpu.SemaphoreType.DMA((2,))],
        compiler_params=pltpu.CompilerParams(vmem_limit_bytes=POST_VMEM),
    )(recv, slot, tokens, q, own, other, odd)


def exchange(rows, experts):
    count, columns = rows.shape
    cut = rows.reshape(experts, count // experts, columns)
    return lax.all_to_all(cut, AXES, split_axis=0, concat_axis=0, tiled=True).reshape(count, columns)


def per_device(tokens, out_grad, expert_ids, router_logits, router_weight, w_in, w_out):
    experts = router_logits.shape[1]
    n_tok, width = tokens.shape
    send, slot, q = prep(
        expert_ids.reshape(1, n_tok), router_logits, tokens, out_grad, router_weight
    )
    recv = exchange(send, experts)
    back, own = expert(recv, w_in, w_out)
    got = exchange(back, experts)
    swap = [(i, i ^ 1) for i in range(lax.axis_size("col"))]
    other = lax.ppermute(own, "col", swap)
    odd = jnp.full((1, 1), lax.axis_index("col") % 2, jnp.int32)
    d_in, d_out = weight_grads(recv, w_in, w_out)
    d_tokens, d_router = post(got, slot, tokens, q, own, other, odd)
    return (d_tokens, d_in, d_out, d_router)


def solution(mesh):
    rows = P(AXES, None)
    cube = P(AXES, None, None)
    return jax.shard_map(
        per_device,
        mesh=mesh,
        in_specs=(rows, rows, P(AXES), rows, rows, cube, cube),
        out_specs=(rows, cube, cube, rows),
        check_vma=False,
    )
```
